32 devices in a mesh: bulk: 8 (over z, x), slab: 4 (over y, core).
Axes of the slice: x: 2, y: 2, z: 4, core: 2. Of those that a mesh axis runs over, the one named last changes fastest.
Arguments:
- pressure: float32 [128, 256, 128], P('bulk', 'slab'), may hold values from -12 to 12
- rhs: float32 [128, 256, 128], P('bulk', 'slab'), may hold values from -48 to 48
- kappa: float32 [128, 256, 128], P('bulk', 'slab'), may hold values from 0.5 to 8
- owner: int32 [4, 8, 1024, 1], P('slab', 'bulk'), may hold values from 0 to 7; in each aligned block of 1024 rows (0 to 1023, 1024 to 2047, ..., all dimensions but the last counted through in order) at most 320 rows name the same one
- coarse_row: int32 [4, 8, 1024], P('slab', 'bulk'), may hold values from 0 to 127
- coarse_leak: float32 [4, 1024, 128], P('slab', 'bulk'), may hold values from 1 to 16
- coarse_link: float32 [4, 1024, 128], P('slab', 'bulk'), may hold values from 1 to 16
Outputs:
- pressure_out: float32 [128, 256, 128], P('bulk', 'slab')
The draws below stay inside these ranges and needn't reach their ends.
Inputs may be any that keep to these rules, and one draw needn't show every extreme that they name: Among the 1024 fine rows of one device, at most 320 name the same owner; in every draw some device gives exactly 320 rows to some owner.
All inputs are finite; a program needn't handle non-finite values.
Results may differ from the reference program's by a relative error of at most 0.00002.
Values sent between devices are 32-bit elements; how exact they have to be, the bound alone decides.
A program may use at most 64 MiB of HBM per device.

```python
import math
import jax
import jax.numpy as jnp
import numpy as np

CX = 16
CY = 64
NZ = 128
SWEEPS = 2
COARSE_SWEEPS = 3
CR = 128
CAP = 320
NX = 128
NY = 256
N_BULK = 8
N_SLAB = 4


def set_ends(entries, stream_key, smallest, top_value):
    index_at = [jax.random.randint(jax.random.fold_in(stream_key, axis), (), 0, length) for axis, length in enumerate(entries.shape)]
    widest = entries.shape.index(max(entries.shape))
    next_to = index_at[:widest] + [(index_at[widest] + 1) % entries.shape[widest]] + index_at[widest + 1:]
    return entries.at[tuple(index_at)].set(smallest).at[tuple(next_to)].set(top_value)


def shard_levels(key, extent, cuts, smallest, high):
    factor_of, own = 1.0, jax.random.fold_in(key, 6)
    for position, shards_of in cuts:
        heights = jnp.exp(jax.random.uniform(jax.random.fold_in(own, position), (shards_of,), jnp.float32, smallest / len(cuts), high / len(cuts)))
        factor_of = factor_of * jnp.repeat(heights, extent[position] // shards_of).reshape([-1 if axis == position else 1 for axis in range(len(extent))])
    return factor_of


def deal_out(key, own, number, rows, amount, top, most, lean):
    ranking = jax.random.permutation(key, amount)
    heavy_load, ordinary = portions_of(amount, rows * top, most, lean, True), portions_of(amount, rows * top, most, lean, False)
    places = jnp.arange(amount)

    def named(tallies, turn):
        used = int((tallies > 0).sum())
        fixed = max(1, used // 4)
        shifted = fixed + (places - fixed + turn * (used - fixed)) % max(1, amount - fixed)
        return jnp.zeros((amount,), jnp.int32).at[ranking[jnp.where(places < fixed, places, shifted)]].set(jnp.asarray(tallies, jnp.int32))

    tallies = jnp.where(number % 4 == 0, named(heavy_load, number // 4), named(ordinary, number - number // 4 - 1))
    mixed = jax.random.permutation(jax.random.fold_in(own, 3), amount)
    donor, sink = mixed[0:amount // 2 * 2:2], mixed[1:amount // 2 * 2:2]
    margin = jnp.minimum(tallies[donor] - 1, most - tallies[sink]) // 2
    margin = jnp.where((donor == ranking[0]) | (sink == ranking[0]) | (tallies[sink] == 0), 0, jnp.maximum(margin, 0))
    shifted = jax.random.randint(jax.random.fold_in(own, 4), (amount // 2,), 0, 1 << 20) % (margin + 1)
    tallies = tallies.at[donor].add(-shifted).at[sink].add(shifted)
    labels = jnp.searchsorted(jnp.cumsum(tallies), jnp.arange(rows * top), side="right").astype(jnp.int32)
    table = labels.reshape(top, rows).T
    table = table[jax.random.permutation(jax.random.fold_in(own, 1), rows)]
    turn = jax.random.randint(jax.random.fold_in(own, 2), (rows, 1), 0, top)
    return jnp.take_along_axis(table, (jnp.arange(top)[None, :] + turn) % top, axis=1)


def portions_of(amount, total, limit, skew, full):
    loads = [(1 << 20) // math.isqrt(rank ** skew) + 1 for rank in range(1, amount + 1)]
    largest = limit if full else min(limit, max(-(-total // amount), total * loads[0] // sum(loads)))
    least = 1 if total - largest >= amount - 1 else 0
    given, surplus = [largest] + [least] * (amount - 1), total - largest - least * (amount - 1)
    while surplus > 0:
        movable = [i for i in range(1, amount) if given[i] < largest] or [i for i in range(1, amount) if given[i] < limit]
        whole, remaining = sum([loads[i] for i in movable]), surplus
        for i in movable:
            more = min(limit - given[i], max(1, remaining * loads[i] // whole), surplus)
            given[i] = given[i] + more
            surplus = surplus - more
    return np.array(given)


def bell_draw(rng, extent, spread, limit, pieces=(), held_as=jnp.bfloat16):
    gain = shard_levels(rng, extent, pieces, -0.22, 0.18) if pieces else 1.0
    values = jax.random.normal(rng, extent, jnp.float32) * spread * gain
    return jnp.minimum(jnp.maximum(values, -limit), limit).astype(held_as)


def setup_inputs(seed: int = 0) -> dict:
    key_of = jax.random.split(jax.random.key(seed), 8)
    pressure = bell_draw(key_of[0], (NX, NY, NZ), 2.0, 12.0, ((0, 8), (1, 4)), jnp.float32)
    rhs = bell_draw(key_of[1], (NX, NY, NZ), 8.0, 48.0, ((0, 8), (1, 4)), jnp.float32)
    kappa = jnp.clip(jnp.exp(math.log(8.0) - 2.7725887 * jax.random.uniform(key_of[2], (NX, NY, NZ), jnp.float32) ** shard_levels(key_of[2], (NX, NY, NZ), ((0, 8), (1, 4)), -0.2, 0.2)), 0.5, 8.0)
    owner_keys = jax.random.split(jax.random.fold_in(key_of[3], 1), N_SLAB * N_BULK * (CX * CY) // (CX * CY))
    owner_turns = jax.random.permutation(jax.random.fold_in(key_of[3], 3), N_SLAB * N_BULK * (CX * CY) // (CX * CY))
    owner = jax.vmap(lambda own, number: deal_out(jax.random.fold_in(key_of[3], 2), own, number, CX * CY, N_BULK, 1, CAP, 1))(owner_keys, owner_turns).reshape((N_SLAB, N_BULK, CX * CY, 1))
    coarse_row = set_ends(jax.random.randint(key_of[4], (N_SLAB, N_BULK, CX * CY), 0, CR), jax.random.fold_in(key_of[4], 1), 0, CR - 1).astype(jnp.int32)
    coarse_leak = jnp.clip(jnp.exp(math.log(16.0) - 2.7725887 * jax.random.uniform(key_of[5], (N_SLAB, N_BULK * CR, NZ), jnp.float32) ** shard_levels(key_of[5], (N_SLAB, N_BULK * CR, NZ), ((0, 4), (1, 8)), -0.2, 0.2)), 1.0, 16.0)
    coarse_link = jnp.clip(jnp.exp(math.log(16.0) - 2.7725887 * jax.random.uniform(key_of[6], (N_SLAB, N_BULK * CR, NZ), jnp.float32) ** shard_levels(key_of[6], (N_SLAB, N_BULK * CR, NZ), ((0, 4), (1, 8)), -0.2, 0.2)), 1.0, 16.0)
    return dict(pressure=pressure, rhs=rhs, kappa=kappa, owner=owner, coarse_row=coarse_row, coarse_leak=coarse_leak, coarse_link=coarse_link)


damping = 0.8


def shift_up(values):
    return jnp.concatenate([values[..., 1:], jnp.zeros_like(values[..., :1])], axis=-1)


def shift_down(values):
    return jnp.concatenate([jnp.zeros_like(values[..., :1]), values[..., :-1]], axis=-1)


def pad_plane(values):
    return jnp.pad(values, ((1, 1), (1, 1), (0, 0)))


def face_set(kappa, kappa_rims):
    west_face = 0.5 * (kappa + kappa_rims[:-2, 1:-1])
    east_face = 0.5 * (kappa + kappa_rims[2:, 1:-1])
    south_face = 0.5 * (kappa + kappa_rims[1:-1, :-2])
    north_face = 0.5 * (kappa + kappa_rims[1:-1, 2:])
    lower_face = 0.5 * (kappa + shift_down(kappa))
    upper_face = 0.5 * (kappa + shift_up(kappa))
    faces = (west_face, east_face, south_face, north_face, lower_face, upper_face)
    diagonal = west_face + east_face + south_face + north_face + lower_face + upper_face
    return faces, diagonal


def operate(field, field_rims, faces):
    west_face, east_face, south_face, north_face, lower_face, upper_face = faces
    result = west_face * (field - field_rims[:-2, 1:-1]) + east_face * (field - field_rims[2:, 1:-1])
    result = result + south_face * (field - field_rims[1:-1, :-2]) + north_face * (field - field_rims[1:-1, 2:])
    result = result + lower_face * (field - shift_down(field)) + upper_face * (field - shift_up(field))
    return result


def coarse_smooth(coarse_rhs, leak, link):
    link_below = shift_down(link)
    cdiag = leak + link + link_below
    correction = jnp.zeros_like(coarse_rhs)
    for sweep_index in range(COARSE_SWEEPS):
        applied = leak * correction + link * (correction - shift_up(correction)) + link_below * (correction - shift_down(correction))
        correction = correction + damping * (coarse_rhs - applied) / cdiag
    return correction


def reference(pressure, rhs, kappa, owner, coarse_row, coarse_leak, coarse_link):
    faces, diagonal = face_set(kappa, pad_plane(kappa))
    field = pressure
    for sweep_index in range(SWEEPS):
        field = field + damping * (rhs - operate(field, pad_plane(field), faces)) / diagonal
    residual = rhs - operate(field, pad_plane(field), faces)
    residual_rows = residual.reshape(N_BULK, CX, N_SLAB, CY, NZ).transpose(2, 0, 1, 3, 4).reshape(N_SLAB * N_BULK * CX * CY, NZ)
    coarse_index = owner.reshape(N_SLAB, N_BULK * CX * CY).astype(jnp.int32) * CR + coarse_row.reshape(N_SLAB, N_BULK * CX * CY).astype(jnp.int32)
    flat_index = (coarse_index + (jnp.arange(N_SLAB, dtype=jnp.int32) * (N_BULK * CR))[:, None]).reshape(-1)
    coarse_rhs = jax.ops.segment_sum(residual_rows, flat_index, num_segments=N_SLAB * N_BULK * CR)
    leak = coarse_leak.reshape(N_SLAB * N_BULK * CR, NZ)
    link = coarse_link.reshape(N_SLAB * N_BULK * CR, NZ)
    correction = coarse_smooth(coarse_rhs, leak, link)
    fine_correction = correction[flat_index].reshape(N_SLAB, N_BULK, CX, CY, NZ).transpose(1, 2, 0, 3, 4).reshape(NX, NY, NZ)
    field = field + fine_correction
    for sweep_index in range(SWEEPS):
        field = field + damping * (rhs - operate(field, pad_plane(field), faces)) / diagonal
    return field
```

```python
import functools

import jax
import jax.numpy as jnp
from jax import lax
from jax.experimental import pallas as pl
from jax.experimental.pallas import tpu as pltpu
from jax.sharding import PartitionSpec as P

SWEEPS = 2
COARSE_SWEEPS = 3
DAMPING = 0.8
PAD = 8
PIECES = 3


def pieces_of(values):
    terms = []
    for index in range(PIECES):
        term = values.astype(jnp.bfloat16)
        terms.append(term)
        if index < PIECES - 1:
            values = values - term.astype(jnp.float32)
    return jnp.concatenate(terms, axis=1)


def joined(product, width):
    total = product[:, :width]
    for index in range(1, PIECES):
        total = total + product[:, index * width : (index + 1) * width]
    return total


def each(count, body):
    if count <= 8:
        for index in range(count):
            body(index)
    else:
        def step(index, carry):
            body(index)
            return carry

        lax.fori_loop(0, count, step, 0)


def kernel(
    nb, ns, key_ref, p_ref, r_ref, k_ref, leak_ref, link_ref, out_ref,
    v, k, rhs, fw, fs, fn, fl, fu, diag, dinv, ysend, yhalo, kysend, kyhalo,
    spread, gather, keycol, rp, part, arrived, corr, acc,
    load_sem, send_sem, recv_sem, ksend_sem, krecv_sem,
    rs_send, rs_recv, ag_send, ag_recv,
):
    cx, cy, nz = out_ref.shape
    cr = leak_ref.shape[0]
    rows = cx * cy
    b = lax.axis_index("bulk")
    s = lax.axis_index("slab")
    body_rows = pl.ds(PAD, cy)

    loads = [
        pltpu.make_async_copy(p_ref, v.at[0, pl.ds(1, cx), body_rows], load_sem.at[0]),
        pltpu.make_async_copy(k_ref, k.at[pl.ds(1, cx), body_rows], load_sem.at[1]),
        pltpu.make_async_copy(r_ref, rhs, load_sem.at[2]),
    ]
    for load in loads:
        load.start()

    has = (b > 0, b < nb - 1, s > 0, s < ns - 1)

    barrier = pltpu.get_barrier_semaphore()

    def greet(j):
        pl.semaphore_signal(
            barrier, inc=1, device_id={"bulk": lax.rem(b + j + 1, nb)},
            device_id_type=pl.DeviceIdType.MESH,
        )

    each(nb - 1, greet)
    for there, step in ((has[2], -1), (has[3], 1)):
        @pl.when(there)
        def _(step=step):
            pl.semaphore_signal(
                barrier, inc=1, device_id={"slab": s + step},
                device_id_type=pl.DeviceIdType.MESH,
            )

    zlane = lax.broadcasted_iota(jnp.int32, (cy, nz), 1)
    first, last = zlane == 0, zlane == nz - 1

    plane0 = jnp.zeros((cy, nz), jnp.float32)
    for there, place in ((has[0], 0), (has[1], cx + 1)):
        @pl.when(jnp.logical_not(there))
        def _(place=place):
            k[place, PAD : PAD + cy] = plane0
            for stage in range(2 * SWEEPS + 1):
                v[stage, place, PAD : PAD + cy] = plane0
    for there, side in ((has[2], 0), (has[3], 1)):
        @pl.when(jnp.logical_not(there))
        def _(side=side):
            kyhalo[side] = jnp.zeros((cx, nz), jnp.float32)
            for stage in range(2 * SWEEPS + 1):
                yhalo[stage, side] = jnp.zeros((cx, nz), jnp.float32)

    lanes = key_ref.shape[1]
    for a in range(key_ref.shape[0]):
        wide = jnp.broadcast_to(key_ref[a : a + 1, :], (lanes, lanes)).astype(jnp.float32)
        keycol[a * lanes : (a + 1) * lanes, :] = wide.T.astype(jnp.int32)

    def onehots(j):
        base = lax.rem(b + j + 1, nb) * cr
        down = lax.broadcasted_iota(jnp.int32, (cr, lanes), 0) + base
        across = lax.broadcasted_iota(jnp.int32, (lanes, cr), 1) + base
        for a in range(key_ref.shape[0]):
            hit = jnp.broadcast_to(key_ref[a : a + 1, :], (cr, lanes)) == down
            spread[j, :, a * lanes : (a + 1) * lanes] = jnp.where(hit, 1.0, 0.0).astype(jnp.bfloat16)
            hit = keycol[a * lanes : (a + 1) * lanes, :cr] == across
            gather[j, a * lanes : (a + 1) * lanes, :] = jnp.where(hit, 1.0, 0.0).astype(jnp.bfloat16)

    def x_copies(ref, sends, recvs, lead):
        def made(source, target, index, step):
            return pltpu.make_async_remote_copy(
                src_ref=ref.at[*lead, source, body_rows], dst_ref=ref.at[*lead, target, body_rows],
                send_sem=sends.at[*lead, index], recv_sem=recvs.at[*lead, index],
                device_id={"bulk": b + step}, device_id_type=pl.DeviceIdType.MESH,
            )
        return made(cx, 0, 0, 1), made(1, cx + 1, 1, -1)

    def y_copies(source, target, sends, recvs, lead):
        def made(side, index, step):
            return pltpu.make_async_remote_copy(
                src_ref=source.at[*lead, side], dst_ref=target.at[*lead, 1 - side],
                send_sem=sends.at[*lead, index], recv_sem=recvs.at[*lead, index],
                device_id={"slab": s + step}, device_id_type=pl.DeviceIdType.MESH,
            )
        return made(1, 2, 1), made(0, 3, -1)

    def copies_of(stage):
        lead = (stage,)
        return x_copies(v, send_sem, recv_sem, lead) + y_copies(ysend, yhalo, send_sem, recv_sem, lead)

    def k_copies():
        return x_copies(k, ksend_sem, krecv_sem, ()) + y_copies(kysend, kyhalo, ksend_sem, krecv_sem, ())

    to = (has[1], has[0], has[3], has[2])
    origin = (has[0], has[1], has[2], has[3])

    def start_all(copies):
        for there, copy in zip(to, copies):
            pl.when(there)(copy.start)

    def recv_all(copies):
        for there, copy in zip(origin, copies):
            pl.when(there)(copy.wait_recv)

    def send_all(copies):
        for there, copy in zip(to, copies):
            pl.when(there)(copy.wait_send)

    def stage_rows(ref, lead, target):
        for x in range(cx):
            target[*lead, 0, x : x + 1] = ref[*lead, x + 1, PAD : PAD + 1]
            target[*lead, 1, x : x + 1] = ref[*lead, x + 1, PAD + cy - 1 : PAD + cy]

    def place_rows(source, lead, ref):
        for x in range(cx):
            ref[*lead, x + 1, PAD - 1 : PAD] = source[*lead, 0, x : x + 1]
            ref[*lead, x + 1, PAD + cy : PAD + cy + 1] = source[*lead, 1, x : x + 1]

    def planes(body):
        def step(x, carry):
            body(x)
            return carry

        lax.fori_loop(0, cx, step, 0)

    loads[0].wait()
    stage_rows(v, (0,), ysend)
    loads[1].wait()
    stage_rows(k, (), kysend)

    pl.semaphore_wait(barrier, nb - 1 + has[2].astype(jnp.int32) + has[3].astype(jnp.int32))

    start_all(k_copies())
    start_all(copies_of(0))
    each(nb, onehots)
    loads[2].wait()
    recv_all(k_copies())
    place_rows(kyhalo, (), k)

    def coefficients(x):
        here = k[x + 1, PAD : PAD + cy]
        west = 0.5 * (here + k[x, PAD : PAD + cy])
        east = 0.5 * (here + k[x + 2, PAD : PAD + cy])
        south = 0.5 * (here + k[x + 1, PAD - 1 : PAD - 1 + cy])
        north = 0.5 * (here + k[x + 1, PAD + 1 : PAD + 1 + cy])
        lower = 0.5 * (here + jnp.where(first, 0.0, pltpu.roll(here, 1, 1)))
        upper = 0.5 * (here + jnp.where(last, 0.0, pltpu.roll(here, nz - 1, 1)))
        total = west + east + south + north + lower + upper
        fw[x] = west
        fw[x + 1] = east
        fs[x] = south
        fn[x] = north
        fl[x] = jnp.where(first, 0.0, lower)
        fu[x] = jnp.where(last, 0.0, upper)
        diag[x] = total
        dinv[x] = DAMPING / total

    planes(coefficients)

    def around(stage, x):
        here = v[stage, x + 1, PAD : PAD + cy]
        total = rhs[x] + fw[x] * v[stage, x, PAD : PAD + cy] + fw[x + 1] * v[stage, x + 2, PAD : PAD + cy]
        total = total + fs[x] * v[stage, x + 1, PAD - 1 : PAD - 1 + cy]
        total = total + fn[x] * v[stage, x + 1, PAD + 1 : PAD + 1 + cy]
        total = total + fl[x] * pltpu.roll(here, 1, 1) + fu[x] * pltpu.roll(here, nz - 1, 1)
        return total, here

    def halo_in(stage):
        recv_all(copies_of(stage))
        place_rows(yhalo, (stage,), v)

    def halo_out(stage):
        stage_rows(v, (stage,), ysend)
        start_all(copies_of(stage))

    def smooth(stage):
        def body(x):
            total, here = around(stage, x)
            v[stage + 1, x + 1, PAD : PAD + cy] = (1 - DAMPING) * here + dinv[x] * total

        planes(body)

    for stage in range(SWEEPS):
        halo_in(stage)
        smooth(stage)
        halo_out(stage + 1)

    halo_in(SWEEPS)

    def residual(x):
        total, here = around(SWEEPS, x)
        rp[pl.ds(pl.multiple_of(x * cy, cy), cy), :] = pieces_of(total - diag[x] * here)

    planes(residual)

    def rs_copy(j):
        return pltpu.make_async_remote_copy(
            src_ref=part.at[j], dst_ref=arrived.at[j],
            send_sem=rs_send.at[j], recv_sem=rs_recv.at[j],
            device_id={"bulk": lax.rem(b + j + 1, nb)}, device_id_type=pl.DeviceIdType.MESH,
        )

    group = 4 if nb % 4 == 0 else 1

    def scatter(g):
        hot = spread[pl.ds(g * group, group)].reshape(group * cr, rows)
        product = jnp.dot(hot, rp[...], preferred_element_type=jnp.float32)
        part[pl.ds(g * group, group)] = joined(product, nz).reshape(group, cr, nz)

    for g in range(nb // group) if nb // group <= 4 else ():
        scatter(g)
        for j in range(g * group, min((g + 1) * group, nb - 1)):
            rs_copy(j).start()
    if nb // group > 4:
        each(nb // group, scatter)
        each(nb - 1, lambda j: rs_copy(j).start())

    zc = lax.broadcasted_iota(jnp.int32, (cr, nz), 1)
    link = link_ref[...]
    below = jnp.where(zc == 0, 0.0, pltpu.roll(link, 1, 1))
    cinv = DAMPING / (leak_ref[...] + link + below)
    above = jnp.where(zc == nz - 1, 0.0, link)

    each(nb - 1, lambda j: rs_copy(j).wait_recv())
    if nb <= 8:
        coarse = part[nb - 1]
        for j in range(nb - 1):
            coarse = coarse + arrived[j]
    else:
        coarse = lax.fori_loop(0, nb - 1, lambda j, total: total + arrived[j], part[nb - 1])

    u = cinv * coarse
    for sweep in range(COARSE_SWEEPS - 1):
        u = (1 - DAMPING) * u + cinv * (
            coarse + above * pltpu.roll(u, nz - 1, 1) + below * pltpu.roll(u, 1, 1)
        )
    corr[nb - 1] = u

    def ag_copy(j):
        return pltpu.make_async_remote_copy(
            src_ref=corr.at[nb - 1], dst_ref=corr.at[nb - 2 - j],
            send_sem=ag_send.at[nb - 2 - j], recv_sem=ag_recv.at[nb - 2 - j],
            device_id={"bulk": lax.rem(b + j + 1, nb)}, device_id_type=pl.DeviceIdType.MESH,
        )

    each(nb - 1, lambda j: ag_copy(j).start())

    def collect(g, fresh):
        values = pieces_of(corr[pl.ds(g * group, group)].reshape(group * cr, nz))
        hot = jnp.concatenate([gather[g * group + i] for i in range(group)], axis=1)
        product = joined(jnp.dot(hot, values, preferred_element_type=jnp.float32), nz)
        acc[...] = product if fresh else acc[...] + product

    if nb // group <= 4:
        for g in range(nb // group):
            for j in range(g * group, min((g + 1) * group, nb - 1)):
                ag_copy(nb - 2 - j).wait_recv()
            collect(g, g == 0)
    else:
        each(nb - 1, lambda j: ag_copy(j).wait_recv())
        acc[...] = jnp.zeros((rows, nz), jnp.float32)
        each(nb // group, lambda g: collect(g, False))

    def corrected(x):
        v[SWEEPS + 1, x + 1, PAD : PAD + cy] = (
            v[SWEEPS, x + 1, PAD : PAD + cy] + acc[pl.ds(pl.multiple_of(x * cy, cy), cy), :]
        )

    planes(corrected)
    halo_out(SWEEPS + 1)

    for stage in range(SWEEPS + 1, 2 * SWEEPS):
        halo_in(stage)
        smooth(stage)
        halo_out(stage + 1)

    halo_in(2 * SWEEPS)

    def finish(x):
        total, here = around(2 * SWEEPS, x)
        out_ref[x] = (1 - DAMPING) * here + dinv[x] * total

    planes(finish)

    send_all(k_copies())
    for stage in range(2 * SWEEPS + 1):
        send_all(copies_of(stage))
    each(nb - 1, lambda j: rs_copy(j).wait_send())
    each(nb - 1, lambda j: ag_copy(j).wait_send())


def per_device(nb, ns, pressure, rhs, kappa, owner, coarse_row, coarse_leak, coarse_link):
    cx, cy, nz = pressure.shape
    cr = coarse_leak.shape[1]
    rows = cx * cy
    lanes = 128
    key = owner.reshape(rows // lanes, lanes) * cr + coarse_row.reshape(rows // lanes, lanes)
    stages = 2 * SWEEPS + 1
    f32, bf16 = jnp.float32, jnp.bfloat16
    block = (cx, cy, nz)
    padded = (cx + 2, cy + 2 * PAD, nz)
    vmem = pl.BlockSpec(memory_space=pltpu.VMEM)
    hbm = pl.BlockSpec(memory_space=pl.ANY)
    dma = pltpu.SemaphoreType.DMA
    return pl.pallas_call(
        functools.partial(kernel, nb, ns),
        out_shape=jax.ShapeDtypeStruct(block, f32),
        in_specs=[vmem, hbm, hbm, hbm, vmem, vmem],
        out_specs=vmem,
        scratch_shapes=[
            pltpu.VMEM((stages,) + padded, f32),
            pltpu.VMEM(padded, f32),
            pltpu.VMEM(block, f32),
            pltpu.VMEM((cx + 1, cy, nz), f32),
            pltpu.VMEM(block, f32),
            pltpu.VMEM(block, f32),
            pltpu.VMEM(block, f32),
            pltpu.VMEM(block, f32),
            pltpu.VMEM(block, f32),
            pltpu.VMEM(block, f32),
            pltpu.VMEM((stages, 2, cx, nz), f32),
            pltpu.VMEM((stages, 2, cx, nz), f32),
            pltpu.VMEM((2, cx, nz), f32),
            pltpu.VMEM((2, cx, nz), f32),
            pltpu.VMEM((nb, cr, rows), bf16),
            pltpu.VMEM((nb, rows, cr), bf16),
            pltpu.VMEM((rows, lanes), jnp.int32),
            pltpu.VMEM((rows, PIECES * nz), bf16),
            pltpu.VMEM((nb, cr, nz), f32),
            pltpu.VMEM((nb, cr, nz), f32),
            pltpu.VMEM((nb, cr, nz), f32),
            pltpu.VMEM((rows, nz), f32),
            dma((3,)),
            dma((stages, 4)),
            dma((stages, 4)),
            dma((4,)),
            dma((4,)),
            dma((nb,)),
            dma((nb,)),
            dma((nb,)),
            dma((nb,)),
        ],
        compiler_params=pltpu.CompilerParams(
            collective_id=0, has_side_effects=True, vmem_limit_bytes=60 * 2**20
        ),
    )(key, pressure, rhs, kappa, coarse_leak[0], coarse_link[0])


def solution(mesh):
    return jax.shard_map(
        functools.partial(per_device, mesh.shape["bulk"], mesh.shape["slab"]),
        mesh=mesh,
        in_specs=(
            P("bulk", "slab", None),
            P("bulk", "slab", None),
            P("bulk", "slab", None),
            P("slab", "bulk", None, None),
            P("slab", "bulk", None),
            P("slab", "bulk", None),
            P("slab", "bulk", None),
        ),
        out_specs=P("bulk", "slab", None),
        check_vma=False,
    )
```

```python
import functools

import jax
import jax.numpy as jnp
from jax import lax
from jax.experimental import pallas as pl
from jax.experimental.pallas import tpu as pltpu
from jax.sharding import PartitionSpec as P

SWEEPS = 2
COARSE_SWEEPS = 3
DAMPING = 0.8
PAD = 8
PIECES = 3


def pieces_of(values):
    terms = []
    for index in range(PIECES):
        term = values.astype(jnp.bfloat16)
        terms.append(term)
        if index < PIECES - 1:
            values = values - term.astype(jnp.float32)
    return jnp.concatenate(terms, axis=1)


def joined(product, width):
    total = product[:, :width]
    for index in range(1, PIECES):
        total = total + product[:, index * width : (index + 1) * width]
    return total


def each(count, body):
    if count <= 8:
        for index in range(count):
            body(index)
    else:
        def step(index, carry):
            body(index)
            return carry

        lax.fori_loop(0, count, step, 0)


def kernel(
    nb, ns, owner_ref, row_ref, p_ref, r_ref, k_ref, leak_hbm, link_hbm, out_hbm,
    key_ref, row_key, leak_ref, link_ref, out_ref, v, k, rhs, fw, fs, fn, fl, fu, diag, dinv, ysend, yhalo, kysend, kyhalo,
    spread, gather, keycol, rp, part, crossed, arrived, corr, acc,
    load_sem, send_sem, recv_sem, ksend_sem, krecv_sem,
    rs_send, rs_recv, ag_send, ag_recv, px_send, px_recv, cx_send, cx_recv, out_sem,
):
    cx, cy, nz = out_ref.shape
    cr = leak_ref.shape[0]
    rows = cx * cy
    b = lax.axis_index("bulk")
    s = lax.axis_index("slab")
    body_rows = pl.ds(PAD, cy)

    loads = [
        pltpu.make_async_copy(p_ref, v.at[0, pl.ds(1, cx), body_rows], load_sem.at[0]),
        pltpu.make_async_copy(k_ref, k.at[pl.ds(1, cx), body_rows], load_sem.at[1]),
        pltpu.make_async_copy(owner_ref, key_ref, load_sem.at[3]),
        pltpu.make_async_copy(row_ref, row_key, load_sem.at[4]),
        pltpu.make_async_copy(r_ref, rhs, load_sem.at[2]),
        pltpu.make_async_copy(leak_hbm, leak_ref, load_sem.at[5]),
        pltpu.make_async_copy(link_hbm, link_ref, load_sem.at[6]),
    ]
    for load in loads:
        load.start()

    has = (b > 0, b < nb - 1, s > 0, s < ns - 1)

    barrier = pltpu.get_barrier_semaphore()

    def greet(j):
        pl.semaphore_signal(
            barrier, inc=1, device_id={"bulk": lax.rem(b + j + 1, nb)},
            device_id_type=pl.DeviceIdType.MESH,
        )

    each(nb - 1, greet)
    for there, step in ((has[2], -1), (has[3], 1)):
        @pl.when(there)
        def _(step=step):
            pl.semaphore_signal(
                barrier, inc=1, device_id={"slab": s + step},
                device_id_type=pl.DeviceIdType.MESH,
            )

    zlane = lax.broadcasted_iota(jnp.int32, (cy, nz), 1)
    first, last = zlane == 0, zlane == nz - 1

    plane0 = jnp.zeros((cy, nz), jnp.float32)
    for there, end in ((has[0], 0), (has[1], cx + 1)):
        @pl.when(jnp.logical_not(there))
        def _(end=end):
            k[end, PAD : PAD + cy] = plane0
            for stage in range(2 * SWEEPS + 1):
                v[stage, end, PAD : PAD + cy] = plane0
    for there, edge in ((has[2], 0), (has[3], 1)):
        @pl.when(jnp.logical_not(there))
        def _(edge=edge):
            kyhalo[edge] = jnp.zeros((cx, nz), jnp.float32)
            for stage in range(2 * SWEEPS + 1):
                yhalo[stage, edge] = jnp.zeros((cx, nz), jnp.float32)

    half = nb // 2
    place, side = b // 2, lax.rem(b, 2)
    other = 1 - side
    lanes = key_ref.shape[1]
    loads[2].wait()
    loads[3].wait()
    key_ref[...] = key_ref[...] * cr + row_key[...]

    def pair_at(q):
        return lax.rem(place + q + 1, half) * 2

    for a in range(key_ref.shape[0]):
        wide = jnp.broadcast_to(key_ref[a : a + 1, :], (lanes, lanes)).astype(jnp.float32)
        keycol[a * lanes : (a + 1) * lanes, :] = wide.T.astype(jnp.int32)

    def onehots(j):
        base = (pair_at(j) + jnp.where(j < half, side, other)) * cr
        down = lax.broadcasted_iota(jnp.int32, (cr, lanes), 0) + base
        across = lax.broadcasted_iota(jnp.int32, (lanes, cr), 1) + base
        for a in range(key_ref.shape[0]):
            hit = jnp.broadcast_to(key_ref[a : a + 1, :], (cr, lanes)) == down
            spread[j, :, a * lanes : (a + 1) * lanes] = jnp.where(hit, 1.0, 0.0).astype(jnp.bfloat16)
            hit = keycol[a * lanes : (a + 1) * lanes, :cr] == across
            gather[j, a * lanes : (a + 1) * lanes, :] = jnp.where(hit, 1.0, 0.0).astype(jnp.bfloat16)

    def x_copies(ref, sends, recvs, lead):
        def made(source, target, index, step):
            return pltpu.make_async_remote_copy(
                src_ref=ref.at[*lead, source, body_rows], dst_ref=ref.at[*lead, target, body_rows],
                send_sem=sends.at[*lead, index], recv_sem=recvs.at[*lead, index],
                device_id={"bulk": b + step}, device_id_type=pl.DeviceIdType.MESH,
            )
        return made(cx, 0, 0, 1), made(1, cx + 1, 1, -1)

    def y_copies(source, target, sends, recvs, lead):
        def made(side, index, step):
            return pltpu.make_async_remote_copy(
                src_ref=source.at[*lead, side], dst_ref=target.at[*lead, 1 - side],
                send_sem=sends.at[*lead, index], recv_sem=recvs.at[*lead, index],
                device_id={"slab": s + step}, device_id_type=pl.DeviceIdType.MESH,
            )
        return made(1, 2, 1), made(0, 3, -1)

    def copies_of(stage):
        lead = (stage,)
        return x_copies(v, send_sem, recv_sem, lead) + y_copies(ysend, yhalo, send_sem, recv_sem, lead)

    def k_copies():
        return x_copies(k, ksend_sem, krecv_sem, ()) + y_copies(kysend, kyhalo, ksend_sem, krecv_sem, ())

    to = (has[1], has[0], has[3], has[2])
    origin = (has[0], has[1], has[2], has[3])

    def start_all(copies):
        for there, copy in zip(to, copies):
            pl.when(there)(copy.start)

    def recv_all(copies):
        for there, copy in zip(origin, copies):
            pl.when(there)(copy.wait_recv)

    def send_all(copies):
        for there, copy in zip(to, copies):
            pl.when(there)(copy.wait_send)

    def stage_rows(ref, lead, target):
        for x in range(cx):
            target[*lead, 0, x : x + 1] = ref[*lead, x + 1, PAD : PAD + 1]
            target[*lead, 1, x : x + 1] = ref[*lead, x + 1, PAD + cy - 1 : PAD + cy]

    def place_rows(source, lead, ref):
        for x in range(cx):
            ref[*lead, x + 1, PAD - 1 : PAD] = source[*lead, 0, x : x + 1]
            ref[*lead, x + 1, PAD + cy : PAD + cy + 1] = source[*lead, 1, x : x + 1]

    def planes(body):
        def step(x, carry):
            body(x)
            return carry

        lax.fori_loop(0, cx, step, 0, unroll=4)

    loads[0].wait()
    stage_rows(v, (0,), ysend)
    loads[1].wait()
    stage_rows(k, (), kysend)

    pl.semaphore_wait(barrier, nb - 1 + has[2].astype(jnp.int32) + has[3].astype(jnp.int32))

    start_all(k_copies())
    start_all(copies_of(0))
    each(nb, onehots)
    loads[4].wait()
    recv_all(k_copies())
    place_rows(kyhalo, (), k)

    def coefficients(x):
        here = k[x + 1, PAD : PAD + cy]
        west = 0.5 * (here + k[x, PAD : PAD + cy])
        east = 0.5 * (here + k[x + 2, PAD : PAD + cy])
        south = 0.5 * (here + k[x + 1, PAD - 1 : PAD - 1 + cy])
        north = 0.5 * (here + k[x + 1, PAD + 1 : PAD + 1 + cy])
        lower = 0.5 * (here + jnp.where(first, 0.0, pltpu.roll(here, 1, 1)))
        upper = 0.5 * (here + jnp.where(last, 0.0, pltpu.roll(here, nz - 1, 1)))
        total = west + east + south + north + lower + upper
        fw[x] = west
        fw[x + 1] = east
        fs[x] = south
        fn[x] = north
        fl[x] = jnp.where(first, 0.0, lower)
        fu[x] = jnp.where(last, 0.0, upper)
        diag[x] = total
        dinv[x] = DAMPING / total

    planes(coefficients)

    def around(stage, x):
        here = v[stage, x + 1, PAD : PAD + cy]
        total = rhs[x] + fw[x] * v[stage, x, PAD : PAD + cy] + fw[x + 1] * v[stage, x + 2, PAD : PAD + cy]
        total = total + fs[x] * v[stage, x + 1, PAD - 1 : PAD - 1 + cy]
        total = total + fn[x] * v[stage, x + 1, PAD + 1 : PAD + 1 + cy]
        total = total + fl[x] * pltpu.roll(here, 1, 1) + fu[x] * pltpu.roll(here, nz - 1, 1)
        return total, here

    def halo_in(stage):
        recv_all(copies_of(stage))
        place_rows(yhalo, (stage,), v)

    def halo_out(stage):
        stage_rows(v, (stage,), ysend)
        start_all(copies_of(stage))

    def smooth(stage):
        def body(x):
            total, here = around(stage, x)
            v[stage + 1, x + 1, PAD : PAD + cy] = (1 - DAMPING) * here + dinv[x] * total

        planes(body)

    for stage in range(SWEEPS):
        halo_in(stage)
        smooth(stage)
        halo_out(stage + 1)

    halo_in(SWEEPS)

    def residual(x):
        total, here = around(SWEEPS, x)
        rp[pl.ds(pl.multiple_of(x * cy, cy), cy), :] = pieces_of(total - diag[x] * here)

    planes(residual)

    def pair_copy(source, target, q, sends, recvs):
        return pltpu.make_async_remote_copy(
            src_ref=source, dst_ref=target, send_sem=sends.at[q], recv_sem=recvs.at[q],
            device_id={"bulk": 2 * place + other}, device_id_type=pl.DeviceIdType.MESH,
        )

    def far_copy(source, target, q, slot, sends, recvs):
        return pltpu.make_async_remote_copy(
            src_ref=source, dst_ref=target, send_sem=sends.at[slot], recv_sem=recvs.at[slot],
            device_id={"bulk": pair_at(q) + side}, device_id_type=pl.DeviceIdType.MESH,
        )

    def px_copy(q):
        return pair_copy(part.at[half + q], crossed.at[q], q, px_send, px_recv)

    def rs_copy(q):
        return far_copy(part.at[q], arrived.at[q], q, q, rs_send, rs_recv)

    group = 4 if half % 4 == 0 else 1

    def scatter(first_slot):
        hot = spread[pl.ds(first_slot, group)].reshape(group * cr, rows)
        product = jnp.dot(hot, rp[...], preferred_element_type=jnp.float32)
        part[pl.ds(first_slot, group)] = joined(product, nz).reshape(group, cr, nz)

    def scatter_across(g):
        scatter(half + g * group)
        each(group, lambda i: px_copy(g * group + i).start())

    each(half // group, scatter_across)
    each(half // group, lambda g: scatter(g * group))

    loads[5].wait()
    loads[6].wait()
    zc = lax.broadcasted_iota(jnp.int32, (cr, nz), 1)
    link = link_ref[...]
    below = jnp.where(zc == 0, 0.0, pltpu.roll(link, 1, 1))
    cinv = DAMPING / (leak_ref[...] + link + below)
    above = jnp.where(zc == nz - 1, 0.0, link)

    def pass_on(q):
        px_copy(q).wait_recv()
        part[q] = part[q] + crossed[q]
        rs_copy(q).start()

    each(half - 1, pass_on)
    px_copy(half - 1).wait_recv()
    coarse = part[half - 1] + crossed[half - 1]
    if half <= 8:
        for q in range(half - 1):
            rs_copy(q).wait_recv()
            coarse = coarse + arrived[q]
    else:
        each(half - 1, lambda q: rs_copy(q).wait_recv())
        coarse = lax.fori_loop(0, half - 1, lambda q, total: total + arrived[q], coarse)

    u = cinv * coarse
    for sweep in range(COARSE_SWEEPS - 1):
        u = (1 - DAMPING) * u + cinv * (
            coarse + above * pltpu.roll(u, nz - 1, 1) + below * pltpu.roll(u, 1, 1)
        )
    corr[half - 1] = u

    def ag_copy(q):
        slot = half - 2 - q
        return far_copy(corr.at[half - 1], corr.at[slot], q, slot, ag_send, ag_recv)

    def cx_copy(q):
        return pair_copy(corr.at[q], corr.at[half + q], q, cx_send, cx_recv)

    each(half - 1, lambda q: ag_copy(q).start())
    cx_copy(half - 1).start()

    def hand_over(q):
        ag_copy(half - 2 - q).wait_recv()
        cx_copy(q).start()

    each(half - 1, hand_over)

    def collect(first_slot, fresh):
        values = pieces_of(corr[pl.ds(first_slot, group)].reshape(group * cr, nz))
        hot = jnp.concatenate([gather[first_slot + i] for i in range(group)], axis=1)
        product = joined(jnp.dot(hot, values, preferred_element_type=jnp.float32), nz)
        acc[...] = product if fresh else acc[...] + product

    if half == group:
        collect(0, True)
    else:
        acc[...] = jnp.zeros((rows, nz), jnp.float32)
        each(half // group, lambda g: collect(g * group, False))
    each(half, lambda q: cx_copy(q).wait_recv())
    each(half // group, lambda g: collect(half + g * group, False))

    def corrected(x):
        v[SWEEPS + 1, x + 1, PAD : PAD + cy] = (
            v[SWEEPS, x + 1, PAD : PAD + cy] + acc[pl.ds(pl.multiple_of(x * cy, cy), cy), :]
        )

    planes(corrected)
    halo_out(SWEEPS + 1)

    for stage in range(SWEEPS + 1, 2 * SWEEPS):
        halo_in(stage)
        smooth(stage)
        halo_out(stage + 1)

    halo_in(2 * SWEEPS)

    def finish(x):
        total, here = around(2 * SWEEPS, x)
        out_ref[x] = (1 - DAMPING) * here + dinv[x] * total

    planes(finish)
    result = pltpu.make_async_copy(out_ref, out_hbm, out_sem)
    result.start()

    send_all(k_copies())
    for stage in range(2 * SWEEPS + 1):
        send_all(copies_of(stage))
    each(half, lambda q: px_copy(q).wait_send())
    each(half, lambda q: cx_copy(q).wait_send())
    each(half - 1, lambda q: rs_copy(q).wait_send())
    each(half - 1, lambda q: ag_copy(q).wait_send())
    result.wait()


def hand_back(parts, source, target, sems):
    size = source.shape[0] // parts
    copies = [
        pltpu.make_async_copy(
            source.at[pl.ds(i * size, size)], target.at[pl.ds(i * size, size)], sems.at[i]
        )
        for i in range(parts)
    ]
    for copy in copies:
        copy.start()
    for copy in copies:
        copy.wait()


def per_device(nb, ns, pressure, rhs, kappa, owner, coarse_row, coarse_leak, coarse_link):
    cx, cy, nz = pressure.shape
    cr = coarse_leak.shape[1]
    rows = cx * cy
    lanes = 128
    keys = (rows // lanes, lanes)
    parts = 4 if cx % 4 == 0 else 1
    stages = 2 * SWEEPS + 1
    f32, bf16 = jnp.float32, jnp.bfloat16
    block = (cx, cy, nz)
    padded = (cx + 2, cy + 2 * PAD, nz)
    vmem = pl.BlockSpec(memory_space=pltpu.VMEM)
    hbm = pl.BlockSpec(memory_space=pl.ANY)
    dma = pltpu.SemaphoreType.DMA
    result = pl.pallas_call(
        functools.partial(kernel, nb, ns),
        out_shape=jax.ShapeDtypeStruct(block, f32),
        in_specs=[hbm] * 7,
        out_specs=hbm,
        scratch_shapes=[
            pltpu.VMEM(keys, jnp.int32),
            pltpu.VMEM(keys, jnp.int32),
            pltpu.VMEM((cr, nz), f32),
            pltpu.VMEM((cr, nz), f32),
            pltpu.VMEM(block, f32),
            pltpu.VMEM((stages,) + padded, f32),
            pltpu.VMEM(padded, f32),
            pltpu.VMEM(block, f32),
            pltpu.VMEM((cx + 1, cy, nz), f32),
            pltpu.VMEM(block, f32),
            pltpu.VMEM(block, f32),
            pltpu.VMEM(block, f32),
            pltpu.VMEM(block, f32),
            pltpu.VMEM(block, f32),
            pltpu.VMEM(block, f32),
            pltpu.VMEM((stages, 2, cx, nz), f32),
            pltpu.VMEM((stages, 2, cx, nz), f32),
            pltpu.VMEM((2, cx, nz), f32),
            pltpu.VMEM((2, cx, nz), f32),
            pltpu.VMEM((nb, cr, rows), bf16),
            pltpu.VMEM((nb, rows, cr), bf16),
            pltpu.VMEM((rows, lanes), jnp.int32),
            pltpu.VMEM((rows, PIECES * nz), bf16),
            pltpu.VMEM((nb, cr, nz), f32),
            pltpu.VMEM((nb // 2, cr, nz), f32),
            pltpu.VMEM((nb // 2, cr, nz), f32),
            pltpu.VMEM((nb, cr, nz), f32),
            pltpu.VMEM((rows, nz), f32),
            dma((7,)),
            dma((stages, 4)),
            dma((stages, 4)),
            dma((4,)),
            dma((4,)),
            dma((nb // 2,)),
            dma((nb // 2,)),
            dma((nb // 2,)),
            dma((nb // 2,)),
            dma((nb // 2,)),
            dma((nb // 2,)),
            dma((nb // 2,)),
            dma((nb // 2,)),
            dma,
        ],
        compiler_params=pltpu.CompilerParams(
            collective_id=0, has_side_effects=True, vmem_limit_bytes=60 * 2**20
        ),
    )(
        owner.reshape(keys), coarse_row.reshape(keys), pressure, rhs, kappa,
        coarse_leak[0], coarse_link[0],
    )
    return pl.pallas_call(
        functools.partial(hand_back, parts),
        out_shape=jax.ShapeDtypeStruct(block, f32),
        in_specs=[hbm],
        out_specs=hbm,
        scratch_shapes=[dma((parts,))],
        compiler_params=pltpu.CompilerParams(vmem_limit_bytes=60 * 2**20),
    )(result)


def solution(mesh):
    return jax.shard_map(
        functools.partial(per_device, mesh.shape["bulk"], mesh.shape["slab"]),
        mesh=mesh,
        in_specs=(
            P("bulk", "slab", None),
            P("bulk", "slab", None),
            P("bulk", "slab", None),
            P("slab", "bulk", None, None),
            P("slab", "bulk", None),
            P("slab", "bulk", None),
            P("slab", "bulk", None),
        ),
        out_specs=P("bulk", "slab", None),
        check_vma=False,
    )
```

```python
import functools

import jax
import jax.numpy as jnp
from jax import lax
from jax.experimental import pallas as pl
from jax.experimental.pallas import tpu as pltpu
from jax.sharding import PartitionSpec as P

SWEEPS = 2
COARSE_SWEEPS = 3
DAMPING = 0.8
PAD = 8
PIECES = 3


def pieces_of(values):
    terms = []
    for index in range(PIECES):
        term = values.astype(jnp.bfloat16)
        terms.append(term)
        if index < PIECES - 1:
            values = values - term.astype(jnp.float32)
    return jnp.concatenate(terms, axis=1)


def joined(product, width):
    total = product[:, :width]
    for index in range(1, PIECES):
        total = total + product[:, index * width : (index + 1) * width]
    return total


def each(count, body):
    if count <= 8:
        for index in range(count):
            body(index)
    else:
        def step(index, carry):
            body(index)
            return carry

        lax.fori_loop(0, count, step, 0)


def kernel(
    nb, ns, owner_ref, row_ref, p_ref, r_ref, k_ref, leak_hbm, link_hbm, out_hbm,
    key_ref, row_key, leak_ref, link_ref, out_ref, v, k, rhs, fw, fs, fn, fl, fu, diag, dinv, ysend, yhalo, kysend, kyhalo,
    spread, gather, keycol, rp, part, crossed, arrived, corr, acc,
    load_sem, send_sem, recv_sem, ksend_sem, krecv_sem,
    rs_send, rs_recv, ag_send, ag_recv, px_send, px_recv, cx_send, cx_recv, out_sem,
):
    cx, cy, nz = out_ref.shape
    cr = leak_ref.shape[0]
    rows = cx * cy
    b = lax.axis_index("bulk")
    s = lax.axis_index("slab")
    body_rows = pl.ds(PAD, cy)

    loads = [
        pltpu.make_async_copy(p_ref, v.at[0, pl.ds(1, cx), body_rows], load_sem.at[0]),
        pltpu.make_async_copy(k_ref, k.at[pl.ds(1, cx), body_rows], load_sem.at[1]),
        pltpu.make_async_copy(owner_ref, key_ref, load_sem.at[3]),
        pltpu.make_async_copy(row_ref, row_key, load_sem.at[4]),
        pltpu.make_async_copy(r_ref, rhs, load_sem.at[2]),
        pltpu.make_async_copy(leak_hbm, leak_ref, load_sem.at[5]),
        pltpu.make_async_copy(link_hbm, link_ref, load_sem.at[6]),
    ]
    for load in loads:
        load.start()

    has = (b > 0, b < nb - 1, s > 0, s < ns - 1)

    barrier = pltpu.get_barrier_semaphore()

    def greet(j):
        pl.semaphore_signal(
            barrier, inc=1, device_id={"bulk": lax.rem(b + j + 1, nb)},
            device_id_type=pl.DeviceIdType.MESH,
        )

    each(nb - 1, greet)
    for there, step in ((has[2], -1), (has[3], 1)):
        @pl.when(there)
        def _(step=step):
            pl.semaphore_signal(
                barrier, inc=1, device_id={"slab": s + step},
                device_id_type=pl.DeviceIdType.MESH,
            )

    zlane = lax.broadcasted_iota(jnp.int32, (cy, nz), 1)
    first, last = zlane == 0, zlane == nz - 1

    plane0 = jnp.zeros((cy, nz), jnp.float32)
    for there, end in ((has[0], 0), (has[1], cx + 1)):
        @pl.when(jnp.logical_not(there))
        def _(end=end):
            k[end, PAD : PAD + cy] = plane0
            for stage in range(2 * SWEEPS + 1):
                v[stage, end, PAD : PAD + cy] = plane0
    for there, edge in ((has[2], 0), (has[3], 1)):
        @pl.when(jnp.logical_not(there))
        def _(edge=edge):
            kyhalo[edge] = jnp.zeros((cx, nz), jnp.float32)
            for stage in range(2 * SWEEPS + 1):
                yhalo[stage, edge] = jnp.zeros((cx, nz), jnp.float32)

    half = nb // 2
    place, side = b // 2, lax.rem(b, 2)
    other = 1 - side
    lanes = key_ref.shape[1]
    loads[2].wait()
    loads[3].wait()
    key_ref[...] = key_ref[...] * cr + row_key[...]

    def pair_at(q):
        return lax.rem(place + q + 1, half) * 2

    for a in range(key_ref.shape[0]):
        wide = jnp.broadcast_to(key_ref[a : a + 1, :], (lanes, lanes)).astype(jnp.float32)
        keycol[a * lanes : (a + 1) * lanes, :] = wide.T.astype(jnp.int32)

    def onehots(j):
        base = (pair_at(j) + jnp.where(j < half, side, other)) * cr
        down = lax.broadcasted_iota(jnp.int32, (cr, lanes), 0) + base
        across = lax.broadcasted_iota(jnp.int32, (lanes, cr), 1) + base
        for a in range(key_ref.shape[0]):
            hit = jnp.broadcast_to(key_ref[a : a + 1, :], (cr, lanes)) == down
            spread[j, :, a * lanes : (a + 1) * lanes] = jnp.where(hit, 1.0, 0.0).astype(jnp.bfloat16)
            hit = keycol[a * lanes : (a + 1) * lanes, :cr] == across
            gather[j, a * lanes : (a + 1) * lanes, :] = jnp.where(hit, 1.0, 0.0).astype(jnp.bfloat16)

    def x_copies(ref, sends, recvs, lead):
        def made(source, target, index, step):
            return pltpu.make_async_remote_copy(
                src_ref=ref.at[*lead, source, body_rows], dst_ref=ref.at[*lead, target, body_rows],
                send_sem=sends.at[*lead, index], recv_sem=recvs.at[*lead, index],
                device_id={"bulk": b + step}, device_id_type=pl.DeviceIdType.MESH,
            )
        return made(cx, 0, 0, 1), made(1, cx + 1, 1, -1)

    def y_copies(source, target, sends, recvs, lead):
        def made(side, index, step):
            return pltpu.make_async_remote_copy(
                src_ref=source.at[*lead, side], dst_ref=target.at[*lead, 1 - side],
                send_sem=sends.at[*lead, index], recv_sem=recvs.at[*lead, index],
                device_id={"slab": s + step}, device_id_type=pl.DeviceIdType.MESH,
            )
        return made(1, 2, 1), made(0, 3, -1)

    def copies_of(stage):
        lead = (stage,)
        return x_copies(v, send_sem, recv_sem, lead) + y_copies(ysend, yhalo, send_sem, recv_sem, lead)

    def k_copies():
        return x_copies(k, ksend_sem, krecv_sem, ()) + y_copies(kysend, kyhalo, ksend_sem, krecv_sem, ())

    to = (has[1], has[0], has[3], has[2])
    origin = (has[0], has[1], has[2], has[3])

    def start_all(copies):
        for there, copy in zip(to, copies):
            pl.when(there)(copy.start)

    def recv_all(copies):
        for there, copy in zip(origin, copies):
            pl.when(there)(copy.wait_recv)

    def send_all(copies):
        for there, copy in zip(to, copies):
            pl.when(there)(copy.wait_send)

    def stage_rows(ref, lead, target):
        for x in range(cx):
            target[*lead, 0, x : x + 1] = ref[*lead, x + 1, PAD : PAD + 1]
            target[*lead, 1, x : x + 1] = ref[*lead, x + 1, PAD + cy - 1 : PAD + cy]

    def place_rows(source, lead, ref):
        for x in range(cx):
            ref[*lead, x + 1, PAD - 1 : PAD] = source[*lead, 0, x : x + 1]
            ref[*lead, x + 1, PAD + cy : PAD + cy + 1] = source[*lead, 1, x : x + 1]

    def planes(body, unroll):
        def step(x, carry):
            body(x)
            return carry

        lax.fori_loop(1, cx - 1, step, 0, unroll=unroll)

    def x_edges(body):
        body(0, 0, cy)
        body(cx - 1, 0, cy)

    def y_edges(body, depth):
        def both(x):
            body(x, 0, depth)
            body(x, cy - depth, depth)

        planes(both, True)

    def interior(body, depth):
        planes(lambda x: body(x, depth, cy - 2 * depth), 2)

    loads[0].wait()
    stage_rows(v, (0,), ysend)
    loads[1].wait()
    stage_rows(k, (), kysend)

    pl.semaphore_wait(barrier, nb - 1 + has[2].astype(jnp.int32) + has[3].astype(jnp.int32))

    start_all(k_copies())
    start_all(copies_of(0))
    each(nb, onehots)
    loads[4].wait()

    def coefficients(x, y, ny):
        own = slice(PAD + y, PAD + y + ny)
        at = slice(y, y + ny)
        here = k[x + 1, own]
        west = 0.5 * (here + k[x, own])
        east = 0.5 * (here + k[x + 2, own])
        south = 0.5 * (here + k[x + 1, PAD + y - 1 : PAD + y - 1 + ny])
        north = 0.5 * (here + k[x + 1, PAD + y + 1 : PAD + y + 1 + ny])
        lower = 0.5 * (here + jnp.where(first[:ny], 0.0, pltpu.roll(here, 1, 1)))
        upper = 0.5 * (here + jnp.where(last[:ny], 0.0, pltpu.roll(here, nz - 1, 1)))
        total = west + east + south + north + lower + upper
        fw[x, at] = west
        fw[x + 1, at] = east
        fs[x, at] = south
        fn[x, at] = north
        fl[x, at] = jnp.where(first[:ny], 0.0, lower)
        fu[x, at] = jnp.where(last[:ny], 0.0, upper)
        diag[x, at] = total
        dinv[x, at] = DAMPING / total

    def around(stage, x, y, ny):
        own = slice(PAD + y, PAD + y + ny)
        at = slice(y, y + ny)
        here = v[stage, x + 1, own]
        total = rhs[x, at] + fw[x, at] * v[stage, x, own] + fw[x + 1, at] * v[stage, x + 2, own]
        total = total + fs[x, at] * v[stage, x + 1, PAD + y - 1 : PAD + y - 1 + ny]
        total = total + fn[x, at] * v[stage, x + 1, PAD + y + 1 : PAD + y + 1 + ny]
        total = total + fl[x, at] * pltpu.roll(here, 1, 1) + fu[x, at] * pltpu.roll(here, nz - 1, 1)
        return total, here

    def smooth(stage):
        def body(x, y, ny):
            total, here = around(stage, x, y, ny)
            at = slice(y, y + ny)
            v[stage + 1, x + 1, PAD + y : PAD + y + ny] = (1 - DAMPING) * here + dinv[x, at] * total

        return body

    def residual(x, y, ny):
        total, here = around(SWEEPS, x, y, ny)
        start = x * cy + y
        if not isinstance(x, int):
            start = pl.multiple_of(start, 2 * PAD)
        rp[pl.ds(start, ny), :] = pieces_of(total - diag[x, y : y + ny] * here)

    def finish(x, y, ny):
        at = slice(y, y + ny)
        total, here = around(2 * SWEEPS, x, y, ny)
        out_ref[x, at] = (1 - DAMPING) * here + dinv[x, at] * total

    def halo_in(stage):
        recv_all(copies_of(stage))
        place_rows(yhalo, (stage,), v)

    def edges_out(body, stage):
        copies = copies_of(stage)
        x_edges(body)
        for there, copy in zip(to[:2], copies[:2]):
            pl.when(there)(copy.start)
        y_edges(body, PAD)
        stage_rows(v, (stage,), ysend)
        for there, copy in zip(to[2:], copies[2:]):
            pl.when(there)(copy.start)

    def sweep_on(stage):
        body = smooth(stage)
        interior(body, PAD)
        halo_in(stage)
        edges_out(body, stage + 1)

    interior(coefficients, PAD)
    interior(smooth(0), PAD)
    recv_all(k_copies())
    place_rows(kyhalo, (), k)
    x_edges(coefficients)
    y_edges(coefficients, PAD)
    halo_in(0)
    edges_out(smooth(0), 1)
    for stage in range(1, SWEEPS):
        sweep_on(stage)

    interior(residual, 2 * PAD)
    halo_in(SWEEPS)
    x_edges(residual)
    y_edges(residual, 2 * PAD)

    def pair_copy(source, target, q, sends, recvs):
        return pltpu.make_async_remote_copy(
            src_ref=source, dst_ref=target, send_sem=sends.at[q], recv_sem=recvs.at[q],
            device_id={"bulk": 2 * place + other}, device_id_type=pl.DeviceIdType.MESH,
        )

    def far_copy(source, target, q, slot, sends, recvs):
        return pltpu.make_async_remote_copy(
            src_ref=source, dst_ref=target, send_sem=sends.at[slot], recv_sem=recvs.at[slot],
            device_id={"bulk": pair_at(q) + side}, device_id_type=pl.DeviceIdType.MESH,
        )

    def px_copy(q):
        return pair_copy(part.at[half + q], crossed.at[q], q, px_send, px_recv)

    def rs_copy(q):
        return far_copy(part.at[q], arrived.at[q], q, q, rs_send, rs_recv)

    group = 2 if half % 2 == 0 else 1

    def scatter(first_slot):
        hot = spread[pl.ds(first_slot, group)].reshape(group * cr, rows)
        product = jnp.dot(hot, rp[...], preferred_element_type=jnp.float32)
        part[pl.ds(first_slot, group)] = joined(product, nz).reshape(group, cr, nz)

    def scatter_across(g):
        scatter(half + g * group)
        each(group, lambda i: px_copy(g * group + i).start())

    each(half // group, scatter_across)
    each(half // group, lambda g: scatter(g * group))

    loads[5].wait()
    loads[6].wait()
    zc = lax.broadcasted_iota(jnp.int32, (cr, nz), 1)
    link = link_ref[...]
    below = jnp.where(zc == 0, 0.0, pltpu.roll(link, 1, 1))
    cinv = DAMPING / (leak_ref[...] + link + below)
    above = jnp.where(zc == nz - 1, 0.0, link)

    def pass_on(q):
        px_copy(q).wait_recv()
        part[q] = part[q] + crossed[q]
        rs_copy(q).start()

    each(half - 1, pass_on)
    px_copy(half - 1).wait_recv()
    coarse = part[half - 1] + crossed[half - 1]
    if half <= 8:
        for q in range(half - 1):
            rs_copy(q).wait_recv()
            coarse = coarse + arrived[q]
    else:
        each(half - 1, lambda q: rs_copy(q).wait_recv())
        coarse = lax.fori_loop(0, half - 1, lambda q, total: total + arrived[q], coarse)

    u = cinv * coarse
    for sweep in range(COARSE_SWEEPS - 1):
        u = (1 - DAMPING) * u + cinv * (
            coarse + above * pltpu.roll(u, nz - 1, 1) + below * pltpu.roll(u, 1, 1)
        )
    corr[half - 1] = u

    def ag_copy(q):
        slot = half - 2 - q
        return far_copy(corr.at[half - 1], corr.at[slot], q, slot, ag_send, ag_recv)

    def cx_copy(q):
        return pair_copy(corr.at[q], corr.at[half + q], q, cx_send, cx_recv)

    each(half - 1, lambda q: ag_copy(q).start())
    cx_copy(half - 1).start()

    def hand_over(i):
        q = half - 2 - i
        ag_copy(i).wait_recv()
        cx_copy(q).start()

    each(half - 1, hand_over)

    def collect(first_slot, fresh):
        values = pieces_of(corr[pl.ds(first_slot, group)].reshape(group * cr, nz))
        hot = jnp.concatenate([gather[first_slot + i] for i in range(group)], axis=1)
        product = joined(jnp.dot(hot, values, preferred_element_type=jnp.float32), nz)
        acc[...] = product if fresh else acc[...] + product

    collect(half - group, True)
    each(half // group - 1, lambda g: collect(half - (g + 2) * group, False))

    def collect_crossed(g):
        low = half - (g + 1) * group
        each(group, lambda i: cx_copy(low + group - 1 - i).wait_recv())
        collect(half + low, False)

    each(half // group, collect_crossed)

    def corrected(x, y, ny):
        start = x * cy + y
        if not isinstance(x, int):
            start = pl.multiple_of(start, PAD)
        own = slice(PAD + y, PAD + y + ny)
        v[SWEEPS + 1, x + 1, own] = v[SWEEPS, x + 1, own] + acc[pl.ds(start, ny), :]

    edges_out(corrected, SWEEPS + 1)
    interior(corrected, PAD)
    for stage in range(SWEEPS + 1, 2 * SWEEPS):
        sweep_on(stage)

    interior(finish, PAD)
    halo_in(2 * SWEEPS)
    x_edges(finish)
    y_edges(finish, PAD)
    result = pltpu.make_async_copy(out_ref, out_hbm, out_sem)
    result.start()

    send_all(k_copies())
    for stage in range(2 * SWEEPS + 1):
        send_all(copies_of(stage))
    each(half, lambda q: px_copy(q).wait_send())
    each(half, lambda q: cx_copy(q).wait_send())
    each(half - 1, lambda q: rs_copy(q).wait_send())
    each(half - 1, lambda q: ag_copy(q).wait_send())
    result.wait()


def hand_back(parts, source, target, held, load_sems, store_sems):
    size = source.shape[0] // parts

    def copies(first, second, sems):
        return [
            pltpu.make_async_copy(
                first.at[pl.ds(i * size, size)], second.at[pl.ds(i * size, size)], sems.at[i]
            )
            for i in range(parts)
        ]

    loads, stores = copies(source, held, load_sems), copies(held, target, store_sems)
    for load in loads:
        load.start()
    for load, store in zip(loads, stores):
        load.wait()
        store.start()
    for store in stores:
        store.wait()


def per_device(nb, ns, pressure, rhs, kappa, owner, coarse_row, coarse_leak, coarse_link):
    cx, cy, nz = pressure.shape
    cr = coarse_leak.shape[1]
    rows = cx * cy
    lanes = 128
    keys = (rows // lanes, lanes)
    parts = 4 if cx % 4 == 0 else 1
    stages = 2 * SWEEPS + 1
    f32, bf16 = jnp.float32, jnp.bfloat16
    block = (cx, cy, nz)
    padded = (cx + 2, cy + 2 * PAD, nz)
    vmem = pl.BlockSpec(memory_space=pltpu.VMEM)
    hbm = pl.BlockSpec(memory_space=pl.ANY)
    dma = pltpu.SemaphoreType.DMA
    result = pl.pallas_call(
        functools.partial(kernel, nb, ns),
        out_shape=jax.ShapeDtypeStruct(block, f32),
        in_specs=[hbm] * 7,
        out_specs=hbm,
        scratch_shapes=[
            pltpu.VMEM(keys, jnp.int32),
            pltpu.VMEM(keys, jnp.int32),
            pltpu.VMEM((cr, nz), f32),
            pltpu.VMEM((cr, nz), f32),
            pltpu.VMEM(block, f32),
            pltpu.VMEM((stages,) + padded, f32),
            pltpu.VMEM(padded, f32),
            pltpu.VMEM(block, f32),
            pltpu.VMEM((cx + 1, cy, nz), f32),
            pltpu.VMEM(block, f32),
            pltpu.VMEM(block, f32),
            pltpu.VMEM(block, f32),
            pltpu.VMEM(block, f32),
            pltpu.VMEM(block, f32),
            pltpu.VMEM(block, f32),
            pltpu.VMEM((stages, 2, cx, nz), f32),
            pltpu.VMEM((stages, 2, cx, nz), f32),
            pltpu.VMEM((2, cx, nz), f32),
            pltpu.VMEM((2, cx, nz), f32),
            pltpu.VMEM((nb, cr, rows), bf16),
            pltpu.VMEM((nb, rows, cr), bf16),
            pltpu.VMEM((rows, lanes), jnp.int32),
            pltpu.VMEM((rows, PIECES * nz), bf16),
            pltpu.VMEM((nb, cr, nz), f32),
            pltpu.VMEM((nb // 2, cr, nz), f32),
            pltpu.VMEM((nb // 2, cr, nz), f32),
            pltpu.VMEM((nb, cr, nz), f32),
            pltpu.VMEM((rows, nz), f32),
            dma((7,)),
            dma((stages, 4)),
            dma((stages, 4)),
            dma((4,)),
            dma((4,)),
            dma((nb // 2,)),
            dma((nb // 2,)),
            dma((nb // 2,)),
            dma((nb // 2,)),
            dma((nb // 2,)),
            dma((nb // 2,)),
            dma((nb // 2,)),
            dma((nb // 2,)),
            dma,
        ],
        compiler_params=pltpu.CompilerParams(
            collective_id=0, has_side_effects=True, vmem_limit_bytes=60 * 2**20
        ),
    )(
        owner.reshape(keys), coarse_row.reshape(keys), pressure, rhs, kappa,
        coarse_leak[0], coarse_link[0],
    )
    return pl.pallas_call(
        functools.partial(hand_back, parts),
        out_shape=jax.ShapeDtypeStruct(block, f32),
        in_specs=[hbm],
        out_specs=hbm,
        scratch_shapes=[pltpu.VMEM(block, f32), dma((parts,)), dma((parts,))],
        compiler_params=pltpu.CompilerParams(vmem_limit_bytes=60 * 2**20),
    )(result)


def solution(mesh):
    return jax.shard_map(
        functools.partial(per_device, mesh.shape["bulk"], mesh.shape["slab"]),
        mesh=mesh,
        in_specs=(
            P("bulk", "slab", None),
            P("bulk", "slab", None),
            P("bulk", "slab", None),
            P("slab", "bulk", None, None),
            P("slab", "bulk", None),
            P("slab", "bulk", None),
            P("slab", "bulk", None),
        ),
        out_specs=P("bulk", "slab", None),
        check_vma=False,
    )
```

```python
import functools

import jax
import jax.numpy as jnp
from jax import lax
from jax.experimental import pallas as pl
from jax.experimental.pallas import tpu as pltpu
from jax.sharding import PartitionSpec as P

SWEEPS = 2
COARSE_SWEEPS = 3
DAMPING = 0.8
PAD = 8
PIECES = 3


def pieces_of(values):
    terms = []
    for index in range(PIECES):
        term = values.astype(jnp.bfloat16)
        terms.append(term)
        if index < PIECES - 1:
            values = values - term.astype(jnp.float32)
    return jnp.concatenate(terms, axis=1)


def joined(product, width):
    total = product[:, :width]
    for index in range(1, PIECES):
        total = total + product[:, index * width : (index + 1) * width]
    return total


def each(count, body):
    if count <= 8:
        for index in range(count):
            body(index)
    else:
        def step(index, carry):
            body(index)
            return carry

        lax.fori_loop(0, count, step, 0)


def kernel(
    nb, ns, owner_ref, row_ref, p_ref, r_ref, k_ref, leak_hbm, link_hbm, out_ref,
    key_ref, row_key, leak_ref, link_ref, v, k, rhs, fw, fs, fn, fl, fu, diag, dinv, ysend, yhalo, kysend, kyhalo,
    spread, gather, keycol, rp, part, crossed, arrived, corr, acc,
    load_sem, send_sem, recv_sem, ksend_sem, krecv_sem,
    rs_send, rs_recv, ag_send, ag_recv, px_send, px_recv, cx_send, cx_recv,
):
    cx, cy, nz = out_ref.shape
    cr = leak_ref.shape[0]
    rows = cx * cy
    b = lax.axis_index("bulk")
    s = lax.axis_index("slab")
    body_rows = pl.ds(PAD, cy)

    loads = [
        pltpu.make_async_copy(p_ref, v.at[0, pl.ds(1, cx), body_rows], load_sem.at[0]),
        pltpu.make_async_copy(k_ref, k.at[pl.ds(1, cx), body_rows], load_sem.at[1]),
        pltpu.make_async_copy(owner_ref, key_ref, load_sem.at[3]),
        pltpu.make_async_copy(row_ref, row_key, load_sem.at[4]),
        pltpu.make_async_copy(r_ref, rhs, load_sem.at[2]),
        pltpu.make_async_copy(leak_hbm, leak_ref, load_sem.at[5]),
        pltpu.make_async_copy(link_hbm, link_ref, load_sem.at[6]),
    ]
    for load in loads:
        load.start()

    has = (b > 0, b < nb - 1, s > 0, s < ns - 1)

    barrier = pltpu.get_barrier_semaphore()

    def greet(j):
        pl.semaphore_signal(
            barrier, inc=1, device_id={"bulk": lax.rem(b + j + 1, nb)},
            device_id_type=pl.DeviceIdType.MESH,
        )

    each(nb - 1, greet)
    for there, step in ((has[2], -1), (has[3], 1)):
        @pl.when(there)
        def _(step=step):
            pl.semaphore_signal(
                barrier, inc=1, device_id={"slab": s + step},
                device_id_type=pl.DeviceIdType.MESH,
            )

    zlane = lax.broadcasted_iota(jnp.int32, (cy, nz), 1)
    first, last = zlane == 0, zlane == nz - 1

    plane0 = jnp.zeros((cy, nz), jnp.float32)
    for there, end in ((has[0], 0), (has[1], cx + 1)):
        @pl.when(jnp.logical_not(there))
        def _(end=end):
            k[end, PAD : PAD + cy] = plane0
            for stage in range(2 * SWEEPS + 1):
                v[stage, end, PAD : PAD + cy] = plane0
    for there, edge in ((has[2], 0), (has[3], 1)):
        @pl.when(jnp.logical_not(there))
        def _(edge=edge):
            kyhalo[edge] = jnp.zeros((cx, nz), jnp.float32)
            for stage in range(2 * SWEEPS + 1):
                yhalo[stage, edge] = jnp.zeros((cx, nz), jnp.float32)

    half = nb // 2
    place, side = b // 2, lax.rem(b, 2)
    other = 1 - side
    lanes = key_ref.shape[1]
    def pair_at(q):
        return lax.rem(place + q + 1, half) * 2


    def base_of(j):
        return (pair_at(j) + jnp.where(j < half, side, other)) * cr

    def spread_onehot(j):
        down = lax.broadcasted_iota(jnp.int32, (cr, lanes), 0) + base_of(j)
        for a in range(key_ref.shape[0]):
            hit = jnp.broadcast_to(key_ref[a : a + 1, :], (cr, lanes)) == down
            spread[j, :, a * lanes : (a + 1) * lanes] = jnp.where(hit, 1.0, 0.0).astype(jnp.bfloat16)

    def key_columns():
        for a in range(key_ref.shape[0]):
            wide = jnp.broadcast_to(key_ref[a : a + 1, :], (lanes, lanes)).astype(jnp.float32)
            keycol[a * lanes : (a + 1) * lanes, :] = wide.T.astype(jnp.int32)

    def gather_onehot(j):
        across = lax.broadcasted_iota(jnp.int32, (lanes, cr), 1) + base_of(j)
        for a in range(key_ref.shape[0]):
            hit = keycol[a * lanes : (a + 1) * lanes, :cr] == across
            gather[j, a * lanes : (a + 1) * lanes, :] = jnp.where(hit, 1.0, 0.0).astype(jnp.bfloat16)

    def x_copies(ref, sends, recvs, lead):
        def made(source, target, index, step):
            return pltpu.make_async_remote_copy(
                src_ref=ref.at[*lead, source, body_rows], dst_ref=ref.at[*lead, target, body_rows],
                send_sem=sends.at[*lead, index], recv_sem=recvs.at[*lead, index],
                device_id={"bulk": b + step}, device_id_type=pl.DeviceIdType.MESH,
            )
        return made(cx, 0, 0, 1), made(1, cx + 1, 1, -1)

    def y_copies(source, target, sends, recvs, lead):
        def made(side, index, step):
            return pltpu.make_async_remote_copy(
                src_ref=source.at[*lead, side], dst_ref=target.at[*lead, 1 - side],
                send_sem=sends.at[*lead, index], recv_sem=recvs.at[*lead, index],
                device_id={"slab": s + step}, device_id_type=pl.DeviceIdType.MESH,
            )
        return made(1, 2, 1), made(0, 3, -1)

    def copies_of(stage):
        lead = (stage,)
        return x_copies(v, send_sem, recv_sem, lead) + y_copies(ysend, yhalo, send_sem, recv_sem, lead)

    def k_copies():
        return x_copies(k, ksend_sem, krecv_sem, ()) + y_copies(kysend, kyhalo, ksend_sem, krecv_sem, ())

    to = (has[1], has[0], has[3], has[2])
    origin = (has[0], has[1], has[2], has[3])

    def start_all(copies):
        for there, copy in zip(to, copies):
            pl.when(there)(copy.start)

    def recv_all(copies):
        for there, copy in zip(origin, copies):
            pl.when(there)(copy.wait_recv)

    def send_all(copies):
        for there, copy in zip(to, copies):
            pl.when(there)(copy.wait_send)

    def stage_rows(ref, lead, target):
        for x in range(cx):
            target[*lead, 0, x : x + 1] = ref[*lead, x + 1, PAD : PAD + 1]
            target[*lead, 1, x : x + 1] = ref[*lead, x + 1, PAD + cy - 1 : PAD + cy]

    def place_rows(source, lead, ref):
        for x in range(cx):
            ref[*lead, x + 1, PAD - 1 : PAD] = source[*lead, 0, x : x + 1]
            ref[*lead, x + 1, PAD + cy : PAD + cy + 1] = source[*lead, 1, x : x + 1]

    def planes(body, unroll):
        def step(x, carry):
            body(x)
            return carry

        lax.fori_loop(1, cx - 1, step, 0, unroll=unroll)

    def x_edges(body):
        body(0, 0, cy)
        body(cx - 1, 0, cy)

    def y_edges(body, depth):
        def both(x):
            body(x, 0, depth)
            body(x, cy - depth, depth)

        planes(both, True)

    def interior(body, depth):
        planes(lambda x: body(x, depth, cy - 2 * depth), 2)

    loads[0].wait()
    stage_rows(v, (0,), ysend)
    loads[1].wait()
    stage_rows(k, (), kysend)

    pl.semaphore_wait(barrier, nb - 1 + has[2].astype(jnp.int32) + has[3].astype(jnp.int32))

    start_all(k_copies())
    start_all(copies_of(0))
    loads[4].wait()

    def coefficients(x, y, ny):
        own = slice(PAD + y, PAD + y + ny)
        at = slice(y, y + ny)
        here = k[x + 1, own]
        west = 0.5 * (here + k[x, own])
        east = 0.5 * (here + k[x + 2, own])
        south = 0.5 * (here + k[x + 1, PAD + y - 1 : PAD + y - 1 + ny])
        north = 0.5 * (here + k[x + 1, PAD + y + 1 : PAD + y + 1 + ny])
        lower = 0.5 * (here + jnp.where(first[:ny], 0.0, pltpu.roll(here, 1, 1)))
        upper = 0.5 * (here + jnp.where(last[:ny], 0.0, pltpu.roll(here, nz - 1, 1)))
        total = west + east + south + north + lower + upper
        fw[x, at] = west
        fw[x + 1, at] = east
        fs[x, at] = south
        fn[x, at] = north
        fl[x, at] = jnp.where(first[:ny], 0.0, lower)
        fu[x, at] = jnp.where(last[:ny], 0.0, upper)
        diag[x, at] = total
        dinv[x, at] = DAMPING / total

    def around(stage, x, y, ny):
        own = slice(PAD + y, PAD + y + ny)
        at = slice(y, y + ny)
        here = v[stage, x + 1, own]
        total = rhs[x, at] + fw[x, at] * v[stage, x, own] + fw[x + 1, at] * v[stage, x + 2, own]
        total = total + fs[x, at] * v[stage, x + 1, PAD + y - 1 : PAD + y - 1 + ny]
        total = total + fn[x, at] * v[stage, x + 1, PAD + y + 1 : PAD + y + 1 + ny]
        total = total + fl[x, at] * pltpu.roll(here, 1, 1) + fu[x, at] * pltpu.roll(here, nz - 1, 1)
        return total, here

    def smooth(stage):
        def body(x, y, ny):
            total, here = around(stage, x, y, ny)
            at = slice(y, y + ny)
            v[stage + 1, x + 1, PAD + y : PAD + y + ny] = (1 - DAMPING) * here + dinv[x, at] * total

        return body

    def residual(x, y, ny):
        total, here = around(SWEEPS, x, y, ny)
        start = x * cy + y
        if not isinstance(x, int):
            start = pl.multiple_of(start, 2 * PAD)
        rp[pl.ds(start, ny), :] = pieces_of(total - diag[x, y : y + ny] * here)

    def finish(x, y, ny):
        at = slice(y, y + ny)
        total, here = around(2 * SWEEPS, x, y, ny)
        out_ref[x, at] = (1 - DAMPING) * here + dinv[x, at] * total

    def halo_in(stage):
        recv_all(copies_of(stage))
        place_rows(yhalo, (stage,), v)

    def edges_out(body, stage):
        copies = copies_of(stage)
        x_edges(body)
        for there, copy in zip(to[:2], copies[:2]):
            pl.when(there)(copy.start)
        y_edges(body, PAD)
        stage_rows(v, (stage,), ysend)
        for there, copy in zip(to[2:], copies[2:]):
            pl.when(there)(copy.start)

    def sweep_on(stage):
        body = smooth(stage)
        interior(body, PAD)
        halo_in(stage)
        edges_out(body, stage + 1)

    interior(coefficients, PAD)
    interior(smooth(0), PAD)
    recv_all(k_copies())
    place_rows(kyhalo, (), k)
    x_edges(coefficients)
    y_edges(coefficients, PAD)
    halo_in(0)
    edges_out(smooth(0), 1)
    loads[2].wait()
    loads[3].wait()
    key_ref[...] = key_ref[...] * cr + row_key[...]
    each(nb, spread_onehot)
    for stage in range(1, SWEEPS):
        sweep_on(stage)

    interior(residual, 2 * PAD)
    key_columns()
    halo_in(SWEEPS)
    x_edges(residual)
    y_edges(residual, 2 * PAD)

    def pair_copy(source, target, q, sends, recvs):
        return pltpu.make_async_remote_copy(
            src_ref=source, dst_ref=target, send_sem=sends.at[q], recv_sem=recvs.at[q],
            device_id={"bulk": 2 * place + other}, device_id_type=pl.DeviceIdType.MESH,
        )

    def far_copy(source, target, q, slot, sends, recvs):
        return pltpu.make_async_remote_copy(
            src_ref=source, dst_ref=target, send_sem=sends.at[slot], recv_sem=recvs.at[slot],
            device_id={"bulk": pair_at(q) + side}, device_id_type=pl.DeviceIdType.MESH,
        )

    def px_copy(q):
        return pair_copy(part.at[half + q], crossed.at[q], q, px_send, px_recv)

    def rs_copy(q):
        return far_copy(part.at[q], arrived.at[q], q, q, rs_send, rs_recv)

    group = 2 if half % 2 == 0 else 1

    def scatter(first_slot):
        hot = spread[pl.ds(first_slot, group)].reshape(group * cr, rows)
        product = jnp.dot(hot, rp[...], preferred_element_type=jnp.float32)
        part[pl.ds(first_slot, group)] = joined(product, nz).reshape(group, cr, nz)

    def scatter_across(g):
        scatter(half + g * group)
        each(group, lambda i: px_copy(g * group + i).start())

    each(half // group, scatter_across)
    each(half // group, lambda g: scatter(g * group))

    loads[5].wait()
    loads[6].wait()
    zc = lax.broadcasted_iota(jnp.int32, (cr, nz), 1)
    link = link_ref[...]
    below = jnp.where(zc == 0, 0.0, pltpu.roll(link, 1, 1))
    cinv = DAMPING / (leak_ref[...] + link + below)
    above = jnp.where(zc == nz - 1, 0.0, link)

    def pass_on(q):
        px_copy(q).wait_recv()
        part[q] = part[q] + crossed[q]
        rs_copy(q).start()

    each(half - 1, pass_on)
    each(half, gather_onehot)
    px_copy(half - 1).wait_recv()
    coarse = part[half - 1] + crossed[half - 1]
    if half <= 8:
        for q in range(half - 1):
            rs_copy(q).wait_recv()
            coarse = coarse + arrived[q]
    else:
        each(half - 1, lambda q: rs_copy(q).wait_recv())
        coarse = lax.fori_loop(0, half - 1, lambda q, total: total + arrived[q], coarse)

    u = cinv * coarse
    for sweep in range(COARSE_SWEEPS - 1):
        u = (1 - DAMPING) * u + cinv * (
            coarse + above * pltpu.roll(u, nz - 1, 1) + below * pltpu.roll(u, 1, 1)
        )
    corr[half - 1] = u

    def ag_copy(q):
        slot = half - 2 - q
        return far_copy(corr.at[half - 1], corr.at[slot], q, slot, ag_send, ag_recv)

    def cx_copy(q):
        return pair_copy(corr.at[q], corr.at[half + q], q, cx_send, cx_recv)

    each(half - 1, lambda q: ag_copy(q).start())
    cx_copy(half - 1).start()
    each(half, lambda q: gather_onehot(half + q))

    def hand_over(i):
        q = half - 2 - i
        ag_copy(i).wait_recv()
        cx_copy(q).start()

    each(half - 1, hand_over)

    def collect(first_slot, fresh):
        values = pieces_of(corr[pl.ds(first_slot, group)].reshape(group * cr, nz))
        hot = jnp.concatenate([gather[first_slot + i] for i in range(group)], axis=1)
        product = joined(jnp.dot(hot, values, preferred_element_type=jnp.float32), nz)
        acc[...] = product if fresh else acc[...] + product

    collect(half - group, True)
    each(half // group - 1, lambda g: collect(half - (g + 2) * group, False))

    def collect_crossed(g):
        low = half - (g + 1) * group
        each(group, lambda i: cx_copy(low + group - 1 - i).wait_recv())
        collect(half + low, False)

    each(half // group, collect_crossed)

    def corrected(x, y, ny):
        start = x * cy + y
        if not isinstance(x, int):
            start = pl.multiple_of(start, PAD)
        own = slice(PAD + y, PAD + y + ny)
        v[SWEEPS + 1, x + 1, own] = v[SWEEPS, x + 1, own] + acc[pl.ds(start, ny), :]

    edges_out(corrected, SWEEPS + 1)
    interior(corrected, PAD)
    for stage in range(SWEEPS + 1, 2 * SWEEPS):
        sweep_on(stage)

    interior(finish, PAD)
    halo_in(2 * SWEEPS)
    x_edges(finish)
    y_edges(finish, PAD)

    send_all(k_copies())
    for stage in range(2 * SWEEPS + 1):
        send_all(copies_of(stage))
    each(half, lambda q: px_copy(q).wait_send())
    each(half, lambda q: cx_copy(q).wait_send())
    each(half - 1, lambda q: rs_copy(q).wait_send())
    each(half - 1, lambda q: ag_copy(q).wait_send())


def hand_back(parts, source, target, sems):
    size = source.shape[0] // parts
    copies = [
        pltpu.make_async_copy(
            source.at[pl.ds(i * size, size)], target.at[pl.ds(i * size, size)], sems.at[i]
        )
        for i in range(parts)
    ]
    for copy in copies:
        copy.start()
    for copy in copies:
        copy.wait()


def per_device(nb, ns, pressure, rhs, kappa, owner, coarse_row, coarse_leak, coarse_link):
    cx, cy, nz = pressure.shape
    cr = coarse_leak.shape[1]
    rows = cx * cy
    lanes = 128
    keys = (rows // lanes, lanes)
    parts = 4 if cx % 4 == 0 else 1
    stages = 2 * SWEEPS + 1
    f32, bf16 = jnp.float32, jnp.bfloat16
    block = (cx, cy, nz)
    padded = (cx + 2, cy + 2 * PAD, nz)
    vmem = pl.BlockSpec(memory_space=pltpu.VMEM)
    hbm = pl.BlockSpec(memory_space=pltpu.HBM)
    dma = pltpu.SemaphoreType.DMA
    result = pl.pallas_call(
        functools.partial(kernel, nb, ns),
        out_shape=pltpu.VMEM(block, f32),
        in_specs=[hbm] * 7,
        out_specs=vmem,
        scratch_shapes=[
            pltpu.VMEM(keys, jnp.int32),
            pltpu.VMEM(keys, jnp.int32),
            pltpu.VMEM((cr, nz), f32),
            pltpu.VMEM((cr, nz), f32),
            pltpu.VMEM((stages,) + padded, f32),
            pltpu.VMEM(padded, f32),
            pltpu.VMEM(block, f32),
            pltpu.VMEM((cx + 1, cy, nz), f32),
            pltpu.VMEM(block, f32),
            pltpu.VMEM(block, f32),
            pltpu.VMEM(block, f32),
            pltpu.VMEM(block, f32),
            pltpu.VMEM(block, f32),
            pltpu.VMEM(block, f32),
            pltpu.VMEM((stages, 2, cx, nz), f32),
            pltpu.VMEM((stages, 2, cx, nz), f32),
            pltpu.VMEM((2, cx, nz), f32),
            pltpu.VMEM((2, cx, nz), f32),
            pltpu.VMEM((nb, cr, rows), bf16),
            pltpu.VMEM((nb, rows, cr), bf16),
            pltpu.VMEM((rows, lanes), jnp.int32),
            pltpu.VMEM((rows, PIECES * nz), bf16),
            pltpu.VMEM((nb, cr, nz), f32),
            pltpu.VMEM((nb // 2, cr, nz), f32),
            pltpu.VMEM((nb // 2, cr, nz), f32),
            pltpu.VMEM((nb, cr, nz), f32),
            pltpu.VMEM((rows, nz), f32),
            dma((7,)),
            dma((stages, 4)),
            dma((stages, 4)),
            dma((4,)),
            dma((4,)),
            dma((nb // 2,)),
            dma((nb // 2,)),
            dma((nb // 2,)),
            dma((nb // 2,)),
            dma((nb // 2,)),
            dma((nb // 2,)),
            dma((nb // 2,)),
            dma((nb // 2,)),
        ],
        compiler_params=pltpu.CompilerParams(
            collective_id=0, has_side_effects=True, vmem_limit_bytes=58 * 2**20
        ),
    )(
        owner.reshape(keys), coarse_row.reshape(keys), pressure, rhs, kappa,
        coarse_leak[0], coarse_link[0],
    )
    return pl.pallas_call(
        functools.partial(hand_back, parts),
        out_shape=jax.ShapeDtypeStruct(block, f32),
        in_specs=[vmem],
        out_specs=hbm,
        scratch_shapes=[dma((parts,))],
        compiler_params=pltpu.CompilerParams(vmem_limit_bytes=16 * 2**20),
    )(result)


def solution(mesh):
    return jax.shard_map(
        functools.partial(per_device, mesh.shape["bulk"], mesh.shape["slab"]),
        mesh=mesh,
        in_specs=(
            P("bulk", "slab", None),
            P("bulk", "slab", None),
            P("bulk", "slab", None),
            P("slab", "bulk", None, None),
            P("slab", "bulk", None),
            P("slab", "bulk", None),
            P("slab", "bulk", None),
        ),
        out_specs=P("bulk", "slab", None),
        check_vma=False,
    )
```

```python
import functools

import jax
import jax.numpy as jnp
from jax import lax
from jax.experimental import pallas as pl
from jax.experimental.pallas import tpu as pltpu
from jax.sharding import PartitionSpec as P

SWEEPS = 2
COARSE_SWEEPS = 3
DAMPING = 0.8
PAD = 8
PIECES = 3


def pieces_of(values):
    terms = []
    for index in range(PIECES):
        term = values.astype(jnp.bfloat16)
        terms.append(term)
        if index < PIECES - 1:
            values = values - term.astype(jnp.float32)
    return jnp.concatenate(terms, axis=1)


def joined(product, width):
    total = product[:, :width]
    for index in range(1, PIECES):
        total = total + product[:, index * width : (index + 1) * width]
    return total


def each(count, body):
    if count <= 8:
        for index in range(count):
            body(index)
    else:
        def step(index, carry):
            body(index)
            return carry

        lax.fori_loop(0, count, step, 0)


def kernel(
    nb, ns, owner_ref, row_ref, p_ref, r_ref, k_ref, leak_hbm, link_hbm, out_ref,
    key_ref, row_key, leak_ref, link_ref, v, k, rhs, fw, fs, fn, fl, fu, diag, dinv, ysend, yhalo, kysend, kyhalo,
    spread, gather, keycol, rp, part, crossed, arrived, corr, acc,
    load_sem, send_sem, recv_sem, ksend_sem, krecv_sem,
    rs_send, rs_recv, ag_send, ag_recv, px_send, px_recv, cx_send, cx_recv,
):
    cx, cy, nz = out_ref.shape
    cr = leak_ref.shape[0]
    rows = cx * cy
    b = lax.axis_index("bulk")
    s = lax.axis_index("slab")
    body_rows = pl.ds(PAD, cy)

    loads = [
        pltpu.make_async_copy(p_ref, v.at[0, pl.ds(1, cx), body_rows], load_sem.at[0]),
        pltpu.make_async_copy(k_ref, k.at[pl.ds(1, cx), body_rows], load_sem.at[1]),
        pltpu.make_async_copy(owner_ref, key_ref, load_sem.at[3]),
        pltpu.make_async_copy(row_ref, row_key, load_sem.at[4]),
        pltpu.make_async_copy(r_ref, rhs, load_sem.at[2]),
        pltpu.make_async_copy(leak_hbm, leak_ref, load_sem.at[5]),
        pltpu.make_async_copy(link_hbm, link_ref, load_sem.at[6]),
    ]
    for load in loads:
        load.start()

    has = (b > 0, b < nb - 1, s > 0, s < ns - 1)

    barrier = pltpu.get_barrier_semaphore()

    def greet(j):
        pl.semaphore_signal(
            barrier, inc=1, device_id={"bulk": lax.rem(b + j + 1, nb)},
            device_id_type=pl.DeviceIdType.MESH,
        )

    each(nb - 1, greet)
    for there, step in ((has[2], -1), (has[3], 1)):
        @pl.when(there)
        def _(step=step):
            pl.semaphore_signal(
                barrier, inc=1, device_id={"slab": s + step},
                device_id_type=pl.DeviceIdType.MESH,
            )

    zlane = lax.broadcasted_iota(jnp.int32, (cy, nz), 1)
    first, last = zlane == 0, zlane == nz - 1

    plane0 = jnp.zeros((cy, nz), jnp.float32)
    for there, end in ((has[0], 0), (has[1], cx + 1)):
        @pl.when(jnp.logical_not(there))
        def _(end=end):
            k[end, PAD : PAD + cy] = plane0
            for stage in range(2 * SWEEPS + 1):
                v[stage, end, PAD : PAD + cy] = plane0
    for there, edge in ((has[2], 0), (has[3], 1)):
        @pl.when(jnp.logical_not(there))
        def _(edge=edge):
            kyhalo[edge] = jnp.zeros((cx, nz), jnp.float32)
            for stage in range(2 * SWEEPS + 1):
                yhalo[stage, edge] = jnp.zeros((cx, nz), jnp.float32)

    half = nb // 2
    cuts = px_send.shape[0] // half
    place, side = b // 2, lax.rem(b, 2)
    other = 1 - side
    lanes = key_ref.shape[1]
    def pair_at(q):
        return lax.rem(place + q + 1, half) * 2


    def base_of(j):
        return (pair_at(j) + jnp.where(j < half, side, other)) * cr

    def spread_onehot(j):
        down = lax.broadcasted_iota(jnp.int32, (cr, lanes), 0) + base_of(j)
        for a in range(key_ref.shape[0]):
            hit = jnp.broadcast_to(key_ref[a : a + 1, :], (cr, lanes)) == down
            spread[j, :, a * lanes : (a + 1) * lanes] = jnp.where(hit, 1.0, 0.0).astype(jnp.bfloat16)

    def key_columns():
        for a in range(key_ref.shape[0]):
            wide = jnp.broadcast_to(key_ref[a : a + 1, :], (lanes, lanes)).astype(jnp.float32)
            keycol[a * lanes : (a + 1) * lanes, :] = wide.T.astype(jnp.int32)

    def gather_onehot(j):
        across = lax.broadcasted_iota(jnp.int32, (lanes, cr), 1) + base_of(j)
        for a in range(key_ref.shape[0]):
            hit = keycol[a * lanes : (a + 1) * lanes, :cr] == across
            gather[j, a * lanes : (a + 1) * lanes, :] = jnp.where(hit, 1.0, 0.0).astype(jnp.bfloat16)

    def x_copies(ref, sends, recvs, lead):
        def made(source, target, index, step):
            return pltpu.make_async_remote_copy(
                src_ref=ref.at[*lead, source, body_rows], dst_ref=ref.at[*lead, target, body_rows],
                send_sem=sends.at[*lead, index], recv_sem=recvs.at[*lead, index],
                device_id={"bulk": b + step}, device_id_type=pl.DeviceIdType.MESH,
            )
        return made(cx, 0, 0, 1), made(1, cx + 1, 1, -1)

    def y_copies(source, target, sends, recvs, lead):
        def made(side, index, step):
            return pltpu.make_async_remote_copy(
                src_ref=source.at[*lead, side], dst_ref=target.at[*lead, 1 - side],
                send_sem=sends.at[*lead, index], recv_sem=recvs.at[*lead, index],
                device_id={"slab": s + step}, device_id_type=pl.DeviceIdType.MESH,
            )
        return made(1, 2, 1), made(0, 3, -1)

    def copies_of(stage):
        lead = (stage,)
        return x_copies(v, send_sem, recv_sem, lead) + y_copies(ysend, yhalo, send_sem, recv_sem, lead)

    def k_copies():
        return x_copies(k, ksend_sem, krecv_sem, ()) + y_copies(kysend, kyhalo, ksend_sem, krecv_sem, ())

    to = (has[1], has[0], has[3], has[2])
    origin = (has[0], has[1], has[2], has[3])

    def start_all(copies):
        for there, copy in zip(to, copies):
            pl.when(there)(copy.start)

    def recv_all(copies):
        for there, copy in zip(origin, copies):
            pl.when(there)(copy.wait_recv)

    def send_all(copies):
        for there, copy in zip(to, copies):
            pl.when(there)(copy.wait_send)

    def stage_rows(ref, lead, target):
        for x in range(cx):
            target[*lead, 0, x : x + 1] = ref[*lead, x + 1, PAD : PAD + 1]
            target[*lead, 1, x : x + 1] = ref[*lead, x + 1, PAD + cy - 1 : PAD + cy]

    def place_rows(source, lead, ref):
        for x in range(cx):
            ref[*lead, x + 1, PAD - 1 : PAD] = source[*lead, 0, x : x + 1]
            ref[*lead, x + 1, PAD + cy : PAD + cy + 1] = source[*lead, 1, x : x + 1]

    def planes(body, unroll):
        def step(x, carry):
            body(x)
            return carry

        lax.fori_loop(1, cx - 1, step, 0, unroll=unroll)

    def x_edges(body):
        body(0, 0, cy)
        body(cx - 1, 0, cy)

    def y_edges(body, depth):
        def both(x):
            body(x, 0, depth)
            body(x, cy - depth, depth)

        planes(both, True)

    def interior(body, depth):
        planes(lambda x: body(x, depth, cy - 2 * depth), 2)

    loads[0].wait()
    stage_rows(v, (0,), ysend)
    loads[1].wait()
    stage_rows(k, (), kysend)

    pl.semaphore_wait(barrier, nb - 1 + has[2].astype(jnp.int32) + has[3].astype(jnp.int32))

    start_all(k_copies())
    start_all(copies_of(0))
    loads[4].wait()

    def coefficients(x, y, ny):
        own = slice(PAD + y, PAD + y + ny)
        at = slice(y, y + ny)
        here = k[x + 1, own]
        west = 0.5 * (here + k[x, own])
        east = 0.5 * (here + k[x + 2, own])
        south = 0.5 * (here + k[x + 1, PAD + y - 1 : PAD + y - 1 + ny])
        north = 0.5 * (here + k[x + 1, PAD + y + 1 : PAD + y + 1 + ny])
        lower = 0.5 * (here + jnp.where(first[:ny], 0.0, pltpu.roll(here, 1, 1)))
        upper = 0.5 * (here + jnp.where(last[:ny], 0.0, pltpu.roll(here, nz - 1, 1)))
        total = west + east + south + north + lower + upper
        fw[x, at] = west
        fw[x + 1, at] = east
        fs[x, at] = south
        fn[x, at] = north
        fl[x, at] = jnp.where(first[:ny], 0.0, lower)
        fu[x, at] = jnp.where(last[:ny], 0.0, upper)
        diag[x, at] = total
        dinv[x, at] = DAMPING / total

    def around(stage, x, y, ny):
        own = slice(PAD + y, PAD + y + ny)
        at = slice(y, y + ny)
        here = v[stage, x + 1, own]
        total = rhs[x, at] + fw[x, at] * v[stage, x, own] + fw[x + 1, at] * v[stage, x + 2, own]
        total = total + fs[x, at] * v[stage, x + 1, PAD + y - 1 : PAD + y - 1 + ny]
        total = total + fn[x, at] * v[stage, x + 1, PAD + y + 1 : PAD + y + 1 + ny]
        total = total + fl[x, at] * pltpu.roll(here, 1, 1) + fu[x, at] * pltpu.roll(here, nz - 1, 1)
        return total, here

    def smooth(stage):
        def body(x, y, ny):
            total, here = around(stage, x, y, ny)
            at = slice(y, y + ny)
            v[stage + 1, x + 1, PAD + y : PAD + y + ny] = (1 - DAMPING) * here + dinv[x, at] * total

        return body

    def residual(x, y, ny):
        total, here = around(SWEEPS, x, y, ny)
        start = x * cy + y
        if not isinstance(x, int):
            start = pl.multiple_of(start, 2 * PAD)
        rp[pl.ds(start, ny), :] = pieces_of(total - diag[x, y : y + ny] * here)

    def finish(x, y, ny):
        at = slice(y, y + ny)
        total, here = around(2 * SWEEPS, x, y, ny)
        out_ref[x, at] = (1 - DAMPING) * here + dinv[x, at] * total

    def halo_in(stage):
        recv_all(copies_of(stage))
        place_rows(yhalo, (stage,), v)

    def edges_out(body, stage):
        copies = copies_of(stage)
        x_edges(body)
        for there, copy in zip(to[:2], copies[:2]):
            pl.when(there)(copy.start)
        y_edges(body, PAD)
        stage_rows(v, (stage,), ysend)
        for there, copy in zip(to[2:], copies[2:]):
            pl.when(there)(copy.start)

    def sweep_on(stage):
        body = smooth(stage)
        interior(body, PAD)
        halo_in(stage)
        edges_out(body, stage + 1)

    interior(coefficients, PAD)
    interior(smooth(0), PAD)
    recv_all(k_copies())
    place_rows(kyhalo, (), k)
    x_edges(coefficients)
    y_edges(coefficients, PAD)
    halo_in(0)
    edges_out(smooth(0), 1)
    loads[2].wait()
    loads[3].wait()
    key_ref[...] = key_ref[...] * cr + row_key[...]
    each(nb, spread_onehot)
    for stage in range(1, SWEEPS):
        sweep_on(stage)

    interior(residual, 2 * PAD)
    key_columns()
    halo_in(SWEEPS)
    x_edges(residual)
    y_edges(residual, 2 * PAD)

    def piece(ref, first_slot, n):
        size = cr // cuts
        return ref.at[first_slot + n // cuts, pl.ds((n % cuts) * size, size)]

    def pair_copy(source, target, n, sends, recvs):
        return pltpu.make_async_remote_copy(
            src_ref=source, dst_ref=target, send_sem=sends.at[n], recv_sem=recvs.at[n],
            device_id={"bulk": 2 * place + other}, device_id_type=pl.DeviceIdType.MESH,
        )

    def far_copy(source, target, q, n, sends, recvs):
        return pltpu.make_async_remote_copy(
            src_ref=source, dst_ref=target, send_sem=sends.at[n], recv_sem=recvs.at[n],
            device_id={"bulk": pair_at(q) + side}, device_id_type=pl.DeviceIdType.MESH,
        )

    def px_copy(n):
        return pair_copy(piece(part, half, n), piece(crossed, 0, n), n, px_send, px_recv)

    def rs_copy(n):
        return far_copy(piece(part, 0, n), piece(arrived, 0, n), n // cuts, n, rs_send, rs_recv)

    group = 2 if half % 2 == 0 else 1

    def scatter(first_slot):
        hot = spread[pl.ds(first_slot, group)].reshape(group * cr, rows)
        product = jnp.dot(hot, rp[...], preferred_element_type=jnp.float32)
        part[pl.ds(first_slot, group)] = joined(product, nz).reshape(group, cr, nz)

    def scatter_across(g):
        scatter(half + g * group)
        each(group * cuts, lambda i: px_copy(g * group * cuts + i).start())

    each(half // group, scatter_across)
    each(half // group, lambda g: scatter(g * group))

    loads[5].wait()
    loads[6].wait()
    zc = lax.broadcasted_iota(jnp.int32, (cr, nz), 1)
    link = link_ref[...]
    below = jnp.where(zc == 0, 0.0, pltpu.roll(link, 1, 1))
    cinv = DAMPING / (leak_ref[...] + link + below)
    above = jnp.where(zc == nz - 1, 0.0, link)

    def pass_on(n):
        px_copy(n).wait_recv()
        rows_of = pl.ds((n % cuts) * (cr // cuts), cr // cuts)
        part[n // cuts, rows_of] = part[n // cuts, rows_of] + crossed[n // cuts, rows_of]
        rs_copy(n).start()

    own = (half - 1) * cuts
    each(own, pass_on)
    each(half, gather_onehot)
    each(cuts, lambda h: px_copy(own + h).wait_recv())
    coarse = part[half - 1] + crossed[half - 1]
    each(own, lambda n: rs_copy(n).wait_recv())
    if half <= 8:
        for q in range(half - 1):
            coarse = coarse + arrived[q]
    else:
        coarse = lax.fori_loop(0, half - 1, lambda q, total: total + arrived[q], coarse)

    u = cinv * coarse
    for sweep in range(COARSE_SWEEPS - 1):
        u = (1 - DAMPING) * u + cinv * (
            coarse + above * pltpu.roll(u, nz - 1, 1) + below * pltpu.roll(u, 1, 1)
        )
    corr[half - 1] = u

    def ag_copy(n):
        q, h = n // cuts, (n % cuts)
        slot = (half - 2 - q) * cuts + h
        return far_copy(piece(corr, 0, own + h), piece(corr, 0, slot), q, slot, ag_send, ag_recv)

    def cx_copy(n):
        return pair_copy(piece(corr, 0, n), piece(corr, half, n), n, cx_send, cx_recv)

    each(own, lambda n: ag_copy(n).start())
    each(cuts, lambda h: cx_copy(own + h).start())
    each(half, lambda q: gather_onehot(half + q))

    def hand_over(n):
        ag_copy(n).wait_recv()
        cx_copy((half - 2 - n // cuts) * cuts + (n % cuts)).start()

    each(own, hand_over)

    def collect(first_slot, fresh):
        values = pieces_of(corr[pl.ds(first_slot, group)].reshape(group * cr, nz))
        hot = jnp.concatenate([gather[first_slot + i] for i in range(group)], axis=1)
        product = joined(jnp.dot(hot, values, preferred_element_type=jnp.float32), nz)
        acc[...] = product if fresh else acc[...] + product

    collect(half - group, True)
    each(half // group - 1, lambda g: collect(half - (g + 2) * group, False))

    def collect_crossed(g):
        low = half - (g + 1) * group
        each(group * cuts, lambda i: cx_copy(low * cuts + i).wait_recv())
        collect(half + low, False)

    each(half // group, collect_crossed)

    def corrected(x, y, ny):
        start = x * cy + y
        if not isinstance(x, int):
            start = pl.multiple_of(start, PAD)
        own = slice(PAD + y, PAD + y + ny)
        v[SWEEPS + 1, x + 1, own] = v[SWEEPS, x + 1, own] + acc[pl.ds(start, ny), :]

    edges_out(corrected, SWEEPS + 1)
    interior(corrected, PAD)
    for stage in range(SWEEPS + 1, 2 * SWEEPS):
        sweep_on(stage)

    interior(finish, PAD)
    halo_in(2 * SWEEPS)
    x_edges(finish)
    y_edges(finish, PAD)

    send_all(k_copies())
    for stage in range(2 * SWEEPS + 1):
        send_all(copies_of(stage))
    each(half * cuts, lambda n: px_copy(n).wait_send())
    each(half * cuts, lambda n: cx_copy(n).wait_send())
    each(own, lambda n: rs_copy(n).wait_send())
    each(own, lambda n: ag_copy(n).wait_send())


def hand_back(parts, source, target, sems):
    size = source.shape[0] // parts
    copies = [
        pltpu.make_async_copy(
            source.at[pl.ds(i * size, size)], target.at[pl.ds(i * size, size)], sems.at[i]
        )
        for i in range(parts)
    ]
    for copy in copies:
        copy.start()
    for copy in copies:
        copy.wait()


def per_device(nb, ns, pressure, rhs, kappa, owner, coarse_row, coarse_leak, coarse_link):
    cx, cy, nz = pressure.shape
    cr = coarse_leak.shape[1]
    rows = cx * cy
    lanes = 128
    cuts = 2 if cr % 16 == 0 else 1
    keys = (rows // lanes, lanes)
    parts = 4 if cx % 4 == 0 else 1
    stages = 2 * SWEEPS + 1
    f32, bf16 = jnp.float32, jnp.bfloat16
    block = (cx, cy, nz)
    padded = (cx + 2, cy + 2 * PAD, nz)
    vmem = pl.BlockSpec(memory_space=pltpu.VMEM)
    hbm = pl.BlockSpec(memory_space=pltpu.HBM)
    dma = pltpu.SemaphoreType.DMA
    result = pl.pallas_call(
        functools.partial(kernel, nb, ns),
        out_shape=pltpu.VMEM(block, f32),
        in_specs=[hbm] * 7,
        out_specs=vmem,
        scratch_shapes=[
            pltpu.VMEM(keys, jnp.int32),
            pltpu.VMEM(keys, jnp.int32),
            pltpu.VMEM((cr, nz), f32),
            pltpu.VMEM((cr, nz), f32),
            pltpu.VMEM((stages,) + padded, f32),
            pltpu.VMEM(padded, f32),
            pltpu.VMEM(block, f32),
            pltpu.VMEM((cx + 1, cy, nz), f32),
            pltpu.VMEM(block, f32),
            pltpu.VMEM(block, f32),
            pltpu.VMEM(block, f32),
            pltpu.VMEM(block, f32),
            pltpu.VMEM(block, f32),
            pltpu.VMEM(block, f32),
            pltpu.VMEM((stages, 2, cx, nz), f32),
            pltpu.VMEM((stages, 2, cx, nz), f32),
            pltpu.VMEM((2, cx, nz), f32),
            pltpu.VMEM((2, cx, nz), f32),
            pltpu.VMEM((nb, cr, rows), bf16),
            pltpu.VMEM((nb, rows, cr), bf16),
            pltpu.VMEM((rows, lanes), jnp.int32),
            pltpu.VMEM((rows, PIECES * nz), bf16),
            pltpu.VMEM((nb, cr, nz), f32),
            pltpu.VMEM((nb // 2, cr, nz), f32),
            pltpu.VMEM((nb // 2, cr, nz), f32),
            pltpu.VMEM((nb, cr, nz), f32),
            pltpu.VMEM((rows, nz), f32),
            dma((7,)),
            dma((stages, 4)),
            dma((stages, 4)),
            dma((4,)),
            dma((4,)),
            dma((nb // 2 * cuts,)),
            dma((nb // 2 * cuts,)),
            dma((nb // 2 * cuts,)),
            dma((nb // 2 * cuts,)),
            dma((nb // 2 * cuts,)),
            dma((nb // 2 * cuts,)),
            dma((nb // 2 * cuts,)),
            dma((nb // 2 * cuts,)),
        ],
        compiler_params=pltpu.CompilerParams(
            collective_id=0, has_side_effects=True, vmem_limit_bytes=58 * 2**20
        ),
    )(
        owner.reshape(keys), coarse_row.reshape(keys), pressure, rhs, kappa,
        coarse_leak[0], coarse_link[0],
    )
    return pl.pallas_call(
        functools.partial(hand_back, parts),
        out_shape=jax.ShapeDtypeStruct(block, f32),
        in_specs=[vmem],
        out_specs=hbm,
        scratch_shapes=[dma((parts,))],
        compiler_params=pltpu.CompilerParams(vmem_limit_bytes=16 * 2**20),
    )(result)


def solution(mesh):
    return jax.shard_map(
        functools.partial(per_device, mesh.shape["bulk"], mesh.shape["slab"]),
        mesh=mesh,
        in_specs=(
            P("bulk", "slab", None),
            P("bulk", "slab", None),
            P("bulk", "slab", None),
            P("slab", "bulk", None, None),
            P("slab", "bulk", None),
            P("slab", "bulk", None),
            P("slab", "bulk", None),
        ),
        out_specs=P("bulk", "slab", None),
        check_vma=False,
    )
```

```python
import functools

import jax
import jax.numpy as jnp
from jax import lax
from jax.experimental import pallas as pl
from jax.experimental.pallas import tpu as pltpu
from jax.sharding import PartitionSpec as P

SWEEPS = 2
COARSE_SWEEPS = 3
DAMPING = 0.8
PAD = 8
PIECES = 3


def pieces_of(values):
    terms = []
    for index in range(PIECES):
        term = values.astype(jnp.bfloat16)
        terms.append(term)
        if index < PIECES - 1:
            values = values - term.astype(jnp.float32)
    return jnp.concatenate(terms, axis=1)


def joined(product, width):
    total = product[:, :width]
    for index in range(1, PIECES):
        total = total + product[:, index * width : (index + 1) * width]
    return total


def each(count, body):
    if count <= 8:
        for index in range(count):
            body(index)
    else:
        def step(index, carry):
            body(index)
            return carry

        lax.fori_loop(0, count, step, 0)


def kernel(
    nb, ns, owner_ref, row_ref, p_ref, r_ref, k_ref, leak_hbm, link_hbm, out_ref,
    key_ref, row_key, leak_ref, link_ref, v, k, rhs, fw, fs, fn, fl, fu, diag, dinv, ysend, yhalo, kysend, kyhalo,
    spread, gather, keycol, rp, part, crossed, arrived, corr, acc,
    load_sem, send_sem, recv_sem, ksend_sem, krecv_sem,
    rs_send, rs_recv, ag_send, ag_recv, px_send, px_recv, cx_send, cx_recv,
):
    cx, cy, nz = out_ref.shape
    cr = leak_ref.shape[0]
    rows = cx * cy
    b = lax.axis_index("bulk")
    s = lax.axis_index("slab")
    body_rows = pl.ds(PAD, cy)

    loads = [
        pltpu.make_async_copy(p_ref, v.at[0, pl.ds(1, cx), body_rows], load_sem.at[0]),
        pltpu.make_async_copy(k_ref, k.at[pl.ds(1, cx), body_rows], load_sem.at[1]),
        pltpu.make_async_copy(owner_ref, key_ref, load_sem.at[3]),
        pltpu.make_async_copy(row_ref, row_key, load_sem.at[4]),
        pltpu.make_async_copy(r_ref, rhs, load_sem.at[2]),
        pltpu.make_async_copy(leak_hbm, leak_ref, load_sem.at[5]),
        pltpu.make_async_copy(link_hbm, link_ref, load_sem.at[6]),
    ]
    for load in loads:
        load.start()

    has = (b > 0, b < nb - 1, s > 0, s < ns - 1)

    barrier = pltpu.get_barrier_semaphore()

    def greet(j):
        pl.semaphore_signal(
            barrier, inc=1, device_id={"bulk": lax.rem(b + j + 1, nb)},
            device_id_type=pl.DeviceIdType.MESH,
        )

    each(nb - 1, greet)
    for there, step in ((has[2], -1), (has[3], 1)):
        @pl.when(there)
        def _(step=step):
            pl.semaphore_signal(
                barrier, inc=1, device_id={"slab": s + step},
                device_id_type=pl.DeviceIdType.MESH,
            )

    zlane = lax.broadcasted_iota(jnp.int32, (cy, nz), 1)
    first, last = zlane == 0, zlane == nz - 1

    plane0 = jnp.zeros((cy, nz), jnp.float32)
    for there, end in ((has[0], 0), (has[1], cx + 1)):
        @pl.when(jnp.logical_not(there))
        def _(end=end):
            k[end, PAD : PAD + cy] = plane0
            for stage in range(2 * SWEEPS + 1):
                v[stage, end, PAD : PAD + cy] = plane0
    for there, edge in ((has[2], 0), (has[3], 1)):
        @pl.when(jnp.logical_not(there))
        def _(edge=edge):
            kyhalo[edge] = jnp.zeros((cx, nz), jnp.float32)
            for stage in range(2 * SWEEPS + 1):
                yhalo[stage, edge] = jnp.zeros((cx, nz), jnp.float32)

    half = nb // 2
    cuts = px_send.shape[0] // half
    place, side = b // 2, lax.rem(b, 2)
    other = 1 - side
    lanes = key_ref.shape[1]
    def pair_at(q):
        return lax.rem(place + q + 1, half) * 2


    def base_of(j):
        return (pair_at(j) + jnp.where(j < half, side, other)) * cr

    def spread_onehot(j):
        down = lax.broadcasted_iota(jnp.int32, (cr, lanes), 0) + base_of(j)
        for a in range(key_ref.shape[0]):
            hit = jnp.broadcast_to(key_ref[a : a + 1, :], (cr, lanes)) == down
            spread[j, :, a * lanes : (a + 1) * lanes] = jnp.where(hit, 1.0, 0.0).astype(jnp.bfloat16)

    def key_columns():
        for a in range(key_ref.shape[0]):
            wide = jnp.broadcast_to(key_ref[a : a + 1, :], (lanes, lanes)).astype(jnp.float32)
            keycol[a * lanes : (a + 1) * lanes, :] = wide.T.astype(jnp.int32)

    def gather_onehot(j):
        across = lax.broadcasted_iota(jnp.int32, (lanes, cr), 1) + base_of(j)
        for a in range(key_ref.shape[0]):
            hit = keycol[a * lanes : (a + 1) * lanes, :cr] == across
            gather[j, a * lanes : (a + 1) * lanes, :] = jnp.where(hit, 1.0, 0.0).astype(jnp.bfloat16)

    def x_copies(ref, sends, recvs, lead):
        def made(source, target, index, step):
            return pltpu.make_async_remote_copy(
                src_ref=ref.at[*lead, source, body_rows], dst_ref=ref.at[*lead, target, body_rows],
                send_sem=sends.at[*lead, index], recv_sem=recvs.at[*lead, index],
                device_id={"bulk": b + step}, device_id_type=pl.DeviceIdType.MESH,
            )
        return made(cx, 0, 0, 1), made(1, cx + 1, 1, -1)

    def y_copies(source, target, sends, recvs, lead):
        def made(side, index, step):
            return pltpu.make_async_remote_copy(
                src_ref=source.at[*lead, side], dst_ref=target.at[*lead, 1 - side],
                send_sem=sends.at[*lead, index], recv_sem=recvs.at[*lead, index],
                device_id={"slab": s + step}, device_id_type=pl.DeviceIdType.MESH,
            )
        return made(1, 2, 1), made(0, 3, -1)

    def copies_of(stage):
        lead = (stage,)
        return x_copies(v, send_sem, recv_sem, lead) + y_copies(ysend, yhalo, send_sem, recv_sem, lead)

    def k_copies():
        return x_copies(k, ksend_sem, krecv_sem, ()) + y_copies(kysend, kyhalo, ksend_sem, krecv_sem, ())

    to = (has[1], has[0], has[3], has[2])
    origin = (has[0], has[1], has[2], has[3])

    def start_all(copies):
        for there, copy in zip(to, copies):
            pl.when(there)(copy.start)

    def recv_all(copies):
        for there, copy in zip(origin, copies):
            pl.when(there)(copy.wait_recv)

    def send_all(copies):
        for there, copy in zip(to, copies):
            pl.when(there)(copy.wait_send)

    def stage_rows(ref, lead, target):
        for x in range(cx):
            target[*lead, 0, x : x + 1] = ref[*lead, x + 1, PAD : PAD + 1]
            target[*lead, 1, x : x + 1] = ref[*lead, x + 1, PAD + cy - 1 : PAD + cy]

    def place_rows(source, lead, ref):
        for x in range(cx):
            ref[*lead, x + 1, PAD - 1 : PAD] = source[*lead, 0, x : x + 1]
            ref[*lead, x + 1, PAD + cy : PAD + cy + 1] = source[*lead, 1, x : x + 1]

    def planes(body, unroll):
        def step(x, carry):
            body(x)
            return carry

        lax.fori_loop(1, cx - 1, step, 0, unroll=unroll)

    def x_edges(body):
        body(0, 0, cy)
        body(cx - 1, 0, cy)

    def y_edges(body, depth):
        def both(x):
            body(x, 0, depth)
            body(x, cy - depth, depth)

        planes(both, True)

    def interior(body, depth):
        planes(lambda x: body(x, depth, cy - 2 * depth), 2)

    loads[0].wait()
    stage_rows(v, (0,), ysend)
    loads[1].wait()
    stage_rows(k, (), kysend)

    pl.semaphore_wait(barrier, nb - 1 + has[2].astype(jnp.int32) + has[3].astype(jnp.int32))

    start_all(k_copies())
    start_all(copies_of(0))
    loads[4].wait()

    def coefficients(x, y, ny):
        own = slice(PAD + y, PAD + y + ny)
        at = slice(y, y + ny)
        here = k[x + 1, own]
        west = 0.5 * (here + k[x, own])
        east = 0.5 * (here + k[x + 2, own])
        south = 0.5 * (here + k[x + 1, PAD + y - 1 : PAD + y - 1 + ny])
        north = 0.5 * (here + k[x + 1, PAD + y + 1 : PAD + y + 1 + ny])
        lower = 0.5 * (here + jnp.where(first[:ny], 0.0, pltpu.roll(here, 1, 1)))
        upper = 0.5 * (here + jnp.where(last[:ny], 0.0, pltpu.roll(here, nz - 1, 1)))
        total = west + east + south + north + lower + upper
        fw[x, at] = west
        fw[x + 1, at] = east
        fs[x, at] = south
        fn[x, at] = north
        fl[x, at] = jnp.where(first[:ny], 0.0, lower)
        fu[x, at] = jnp.where(last[:ny], 0.0, upper)
        diag[x, at] = total
        dinv[x, at] = DAMPING / total

    def around(stage, x, y, ny):
        own = slice(PAD + y, PAD + y + ny)
        at = slice(y, y + ny)
        here = v[stage, x + 1, own]
        total = rhs[x, at] + fw[x, at] * v[stage, x, own] + fw[x + 1, at] * v[stage, x + 2, own]
        total = total + fs[x, at] * v[stage, x + 1, PAD + y - 1 : PAD + y - 1 + ny]
        total = total + fn[x, at] * v[stage, x + 1, PAD + y + 1 : PAD + y + 1 + ny]
        total = total + fl[x, at] * pltpu.roll(here, 1, 1) + fu[x, at] * pltpu.roll(here, nz - 1, 1)
        return total, here

    def smooth(stage):
        def body(x, y, ny):
            total, here = around(stage, x, y, ny)
            at = slice(y, y + ny)
            v[stage + 1, x + 1, PAD + y : PAD + y + ny] = (1 - DAMPING) * here + dinv[x, at] * total

        return body

    def residual(x, y, ny):
        total, here = around(SWEEPS, x, y, ny)
        start = x * cy + y
        if not isinstance(x, int):
            start = pl.multiple_of(start, 2 * PAD)
        rp[pl.ds(start, ny), :] = pieces_of(total - diag[x, y : y + ny] * here)

    def finish(x, y, ny):
        at = slice(y, y + ny)
        total, here = around(2 * SWEEPS, x, y, ny)
        out_ref[x, at] = (1 - DAMPING) * here + dinv[x, at] * total

    def halo_in(stage):
        recv_all(copies_of(stage))
        place_rows(yhalo, (stage,), v)

    def edges_out(body, stage):
        copies = copies_of(stage)
        x_edges(body)
        for there, copy in zip(to[:2], copies[:2]):
            pl.when(there)(copy.start)
        y_edges(body, PAD)
        stage_rows(v, (stage,), ysend)
        for there, copy in zip(to[2:], copies[2:]):
            pl.when(there)(copy.start)

    def sweep_on(stage):
        body = smooth(stage)
        interior(body, PAD)
        halo_in(stage)
        edges_out(body, stage + 1)

    interior(coefficients, PAD)
    interior(smooth(0), PAD)
    recv_all(k_copies())
    place_rows(kyhalo, (), k)
    x_edges(coefficients)
    y_edges(coefficients, PAD)
    halo_in(0)
    edges_out(smooth(0), 1)
    loads[2].wait()
    loads[3].wait()
    key_ref[...] = key_ref[...] * cr + row_key[...]
    each(nb, spread_onehot)
    for stage in range(1, SWEEPS):
        sweep_on(stage)

    interior(residual, 2 * PAD)
    key_columns()
    halo_in(SWEEPS)
    x_edges(residual)
    y_edges(residual, 2 * PAD)

    def piece(ref, first_slot, n):
        size = cr // cuts
        return ref.at[first_slot + n // cuts, pl.ds((n % cuts) * size, size)]

    def pair_copy(source, target, n, sends, recvs):
        return pltpu.make_async_remote_copy(
            src_ref=source, dst_ref=target, send_sem=sends.at[n], recv_sem=recvs.at[n],
            device_id={"bulk": 2 * place + other}, device_id_type=pl.DeviceIdType.MESH,
        )

    def far_copy(source, target, q, n, sends, recvs):
        return pltpu.make_async_remote_copy(
            src_ref=source, dst_ref=target, send_sem=sends.at[n], recv_sem=recvs.at[n],
            device_id={"bulk": pair_at(q) + side}, device_id_type=pl.DeviceIdType.MESH,
        )

    def px_copy(n):
        return pair_copy(piece(part, half, n), piece(crossed, 0, n), n, px_send, px_recv)

    def rs_copy(n):
        return far_copy(piece(part, 0, n), piece(arrived, 0, n), n // cuts, n, rs_send, rs_recv)

    group = 2 if half % 2 == 0 else 1

    def scatter(first_slot):
        hot = spread[pl.ds(first_slot, group)].reshape(group * cr, rows)
        product = jnp.dot(hot, rp[...], preferred_element_type=jnp.float32)
        part[pl.ds(first_slot, group)] = joined(product, nz).reshape(group, cr, nz)

    def scatter_across(g):
        scatter(half + g * group)
        each(group * cuts, lambda i: px_copy(g * group * cuts + i).start())

    each(half // group, scatter_across)
    each(half // group, lambda g: scatter(g * group))

    loads[5].wait()
    loads[6].wait()
    zc = lax.broadcasted_iota(jnp.int32, (cr, nz), 1)
    link = link_ref[...]
    below = jnp.where(zc == 0, 0.0, pltpu.roll(link, 1, 1))
    cinv = DAMPING / (leak_ref[...] + link + below)
    above = jnp.where(zc == nz - 1, 0.0, link)

    def pass_on(n):
        px_copy(n).wait_recv()
        rows_of = pl.ds((n % cuts) * (cr // cuts), cr // cuts)
        part[n // cuts, rows_of] = part[n // cuts, rows_of] + crossed[n // cuts, rows_of]
        rs_copy(n).start()

    own = (half - 1) * cuts
    each(own, pass_on)
    each(half, gather_onehot)
    each(cuts, lambda h: px_copy(own + h).wait_recv())
    coarse = part[half - 1] + crossed[half - 1]
    each(own, lambda n: rs_copy(n).wait_recv())
    if half <= 8:
        for q in range(half - 1):
            coarse = coarse + arrived[q]
    else:
        coarse = lax.fori_loop(0, half - 1, lambda q, total: total + arrived[q], coarse)

    u = cinv * coarse
    for sweep in range(COARSE_SWEEPS - 1):
        u = (1 - DAMPING) * u + cinv * (
            coarse + above * pltpu.roll(u, nz - 1, 1) + below * pltpu.roll(u, 1, 1)
        )
    corr[half - 1] = u

    def ag_copy(n):
        q, h = n // cuts, (n % cuts)
        slot = (half - 2 - q) * cuts + h
        return far_copy(piece(corr, 0, own + h), piece(corr, 0, slot), q, slot, ag_send, ag_recv)

    def cx_copy(n):
        return pair_copy(piece(corr, 0, n), piece(corr, half, n), n, cx_send, cx_recv)

    each(cuts, lambda h: cx_copy(own + h).start())
    each(own, lambda n: ag_copy(n).start())
    each(half, lambda q: gather_onehot(half + q))

    def hand_over(n):
        ag_copy(n).wait_recv()
        cx_copy((half - 2 - n // cuts) * cuts + (n % cuts)).start()

    each(own, hand_over)

    def collect(first_slot, fresh, spans=((0, rows),), between=()):
        values = pieces_of(corr[pl.ds(first_slot, group)].reshape(group * cr, nz))
        for index, (low, high) in enumerate(spans):
            hot = jnp.concatenate([gather[first_slot + i, low:high] for i in range(group)], axis=1)
            product = joined(jnp.dot(hot, values, preferred_element_type=jnp.float32), nz)
            acc[low:high] = product if fresh else acc[low:high] + product
            if index < len(between):
                between[index]()

    collect(half - group, True)
    each(half // group - 1, lambda g: collect(half - (g + 2) * group, False))

    def collect_crossed(g, *order):
        low = half - (g + 1) * group
        each(group * cuts, lambda i: cx_copy(low * cuts + i).wait_recv())
        collect(half + low, False, *order)

    each(half // group - 1, collect_crossed)

    def corrected(x, y, ny):
        start = x * cy + y
        if not isinstance(x, int):
            start = pl.multiple_of(start, PAD)
        own = slice(PAD + y, PAD + y + ny)
        v[SWEEPS + 1, x + 1, own] = v[SWEEPS, x + 1, own] + acc[pl.ds(start, ny), :]

    copies = copies_of(SWEEPS + 1)

    def send_x():
        x_edges(corrected)
        for there, copy in zip(to[:2], copies[:2]):
            pl.when(there)(copy.start)

    collect_crossed(
        half // group - 1, ((0, cy), (rows - cy, rows), (cy, rows - cy)), (lambda: None, send_x)
    )
    y_edges(corrected, PAD)
    stage_rows(v, (SWEEPS + 1,), ysend)
    for there, copy in zip(to[2:], copies[2:]):
        pl.when(there)(copy.start)
    interior(corrected, PAD)
    for stage in range(SWEEPS + 1, 2 * SWEEPS):
        sweep_on(stage)

    interior(finish, PAD)
    halo_in(2 * SWEEPS)
    x_edges(finish)
    y_edges(finish, PAD)

    send_all(k_copies())
    for stage in range(2 * SWEEPS + 1):
        send_all(copies_of(stage))
    each(half * cuts, lambda n: px_copy(n).wait_send())
    each(half * cuts, lambda n: cx_copy(n).wait_send())
    each(own, lambda n: rs_copy(n).wait_send())
    each(own, lambda n: ag_copy(n).wait_send())


def hand_back(parts, source, target, sems):
    size = source.shape[0] // parts
    copies = [
        pltpu.make_async_copy(
            source.at[pl.ds(i * size, size)], target.at[pl.ds(i * size, size)], sems.at[i]
        )
        for i in range(parts)
    ]
    for copy in copies:
        copy.start()
    for copy in copies:
        copy.wait()


def per_device(nb, ns, pressure, rhs, kappa, owner, coarse_row, coarse_leak, coarse_link):
    cx, cy, nz = pressure.shape
    cr = coarse_leak.shape[1]
    rows = cx * cy
    lanes = 128
    cuts = 2 if cr % 16 == 0 else 1
    keys = (rows // lanes, lanes)
    parts = 4 if cx % 4 == 0 else 1
    stages = 2 * SWEEPS + 1
    f32, bf16 = jnp.float32, jnp.bfloat16
    block = (cx, cy, nz)
    padded = (cx + 2, cy + 2 * PAD, nz)
    vmem = pl.BlockSpec(memory_space=pltpu.VMEM)
    hbm = pl.BlockSpec(memory_space=pltpu.HBM)
    dma = pltpu.SemaphoreType.DMA
    result = pl.pallas_call(
        functools.partial(kernel, nb, ns),
        out_shape=pltpu.VMEM(block, f32),
        in_specs=[hbm] * 7,
        out_specs=vmem,
        scratch_shapes=[
            pltpu.VMEM(keys, jnp.int32),
            pltpu.VMEM(keys, jnp.int32),
            pltpu.VMEM((cr, nz), f32),
            pltpu.VMEM((cr, nz), f32),
            pltpu.VMEM((stages,) + padded, f32),
            pltpu.VMEM(padded, f32),
            pltpu.VMEM(block, f32),
            pltpu.VMEM((cx + 1, cy, nz), f32),
            pltpu.VMEM(block, f32),
            pltpu.VMEM(block, f32),
            pltpu.VMEM(block, f32),
            pltpu.VMEM(block, f32),
            pltpu.VMEM(block, f32),
            pltpu.VMEM(block, f32),
            pltpu.VMEM((stages, 2, cx, nz), f32),
            pltpu.VMEM((stages, 2, cx, nz), f32),
            pltpu.VMEM((2, cx, nz), f32),
            pltpu.VMEM((2, cx, nz), f32),
            pltpu.VMEM((nb, cr, rows), bf16),
            pltpu.VMEM((nb, rows, cr), bf16),
            pltpu.VMEM((rows, lanes), jnp.int32),
            pltpu.VMEM((rows, PIECES * nz), bf16),
            pltpu.VMEM((nb, cr, nz), f32),
            pltpu.VMEM((nb // 2, cr, nz), f32),
            pltpu.VMEM((nb // 2, cr, nz), f32),
            pltpu.VMEM((nb, cr, nz), f32),
            pltpu.VMEM((rows, nz), f32),
            dma((7,)),
            dma((stages, 4)),
            dma((stages, 4)),
            dma((4,)),
            dma((4,)),
            dma((nb // 2 * cuts,)),
            dma((nb // 2 * cuts,)),
            dma((nb // 2 * cuts,)),
            dma((nb // 2 * cuts,)),
            dma((nb // 2 * cuts,)),
            dma((nb // 2 * cuts,)),
            dma((nb // 2 * cuts,)),
            dma((nb // 2 * cuts,)),
        ],
        compiler_params=pltpu.CompilerParams(
            collective_id=0, has_side_effects=True, vmem_limit_bytes=58 * 2**20
        ),
    )(
        owner.reshape(keys), coarse_row.reshape(keys), pressure, rhs, kappa,
        coarse_leak[0], coarse_link[0],
    )
    return pl.pallas_call(
        functools.partial(hand_back, parts),
        out_shape=jax.ShapeDtypeStruct(block, f32),
        in_specs=[vmem],
        out_specs=hbm,
        scratch_shapes=[dma((parts,))],
        compiler_params=pltpu.CompilerParams(vmem_limit_bytes=16 * 2**20),
    )(result)


def solution(mesh):
    return jax.shard_map(
        functools.partial(per_device, mesh.shape["bulk"], mesh.shape["slab"]),
        mesh=mesh,
        in_specs=(
            P("bulk", "slab", None),
            P("bulk", "slab", None),
            P("bulk", "slab", None),
            P("slab", "bulk", None, None),
            P("slab", "bulk", None),
            P("slab", "bulk", None),
            P("slab", "bulk", None),
        ),
        out_specs=P("bulk", "slab", None),
        check_vma=False,
    )
```

```python
import functools

import jax
import jax.numpy as jnp
from jax import lax
from jax.experimental import pallas as pl
from jax.experimental.pallas import tpu as pltpu
from jax.sharding import PartitionSpec as P

SWEEPS = 2
COARSE_SWEEPS = 3
DAMPING = 0.8
PAD = 8
PIECES = 3


def pieces_of(values):
    terms = []
    for index in range(PIECES):
        term = values.astype(jnp.bfloat16)
        terms.append(term)
        if index < PIECES - 1:
            values = values - term.astype(jnp.float32)
    return jnp.concatenate(terms, axis=1)


def joined(product, width):
    total = product[:, :width]
    for index in range(1, PIECES):
        total = total + product[:, index * width : (index + 1) * width]
    return total


def each(count, body):
    if count <= 8:
        for index in range(count):
            body(index)
    else:
        def step(index, carry):
            body(index)
            return carry

        lax.fori_loop(0, count, step, 0)


def kernel(
    nb, ns, owner_ref, row_ref, p_ref, r_ref, k_ref, leak_hbm, link_hbm, out_ref,
    key_ref, row_key, leak_ref, link_ref, v, k, rhs, fw, fs, fn, fl, fu, diag, dinv, ysend, yhalo, kysend, kyhalo,
    spread, gather, keycol, rp, part, crossed, arrived, corr, acc,
    load_sem, send_sem, recv_sem, ksend_sem, krecv_sem,
    rs_send, rs_recv, ag_send, ag_recv, px_send, px_recv, cx_send, cx_recv,
):
    cx, cy, nz = out_ref.shape
    cr = leak_ref.shape[0]
    rows = cx * cy
    b = lax.axis_index("bulk")
    s = lax.axis_index("slab")
    body_rows = pl.ds(PAD, cy)

    loads = [
        pltpu.make_async_copy(p_ref, v.at[0, pl.ds(1, cx), body_rows], load_sem.at[0]),
        pltpu.make_async_copy(k_ref, k.at[pl.ds(1, cx), body_rows], load_sem.at[1]),
        pltpu.make_async_copy(owner_ref, key_ref, load_sem.at[3]),
        pltpu.make_async_copy(row_ref, row_key, load_sem.at[4]),
        pltpu.make_async_copy(r_ref, rhs, load_sem.at[2]),
        pltpu.make_async_copy(leak_hbm, leak_ref, load_sem.at[5]),
        pltpu.make_async_copy(link_hbm, link_ref, load_sem.at[6]),
    ]
    for load in loads:
        load.start()

    has = (b > 0, b < nb - 1, s > 0, s < ns - 1)

    barrier = pltpu.get_barrier_semaphore()

    def greet(j):
        pl.semaphore_signal(
            barrier, inc=1, device_id={"bulk": lax.rem(b + j + 1, nb)},
            device_id_type=pl.DeviceIdType.MESH,
        )

    each(nb - 1, greet)
    for there, step in ((has[2], -1), (has[3], 1)):
        @pl.when(there)
        def _(step=step):
            pl.semaphore_signal(
                barrier, inc=1, device_id={"slab": s + step},
                device_id_type=pl.DeviceIdType.MESH,
            )

    zlane = lax.broadcasted_iota(jnp.int32, (cy, nz), 1)
    first, last = zlane == 0, zlane == nz - 1

    plane0 = jnp.zeros((cy, nz), jnp.float32)
    for there, end in ((has[0], 0), (has[1], cx + 1)):
        @pl.when(jnp.logical_not(there))
        def _(end=end):
            k[end, PAD : PAD + cy] = plane0
            for stage in range(2 * SWEEPS + 1):
                v[stage, end, PAD : PAD + cy] = plane0
    for there, edge in ((has[2], 0), (has[3], 1)):
        @pl.when(jnp.logical_not(there))
        def _(edge=edge):
            kyhalo[edge] = jnp.zeros((cx, nz), jnp.float32)
            for stage in range(2 * SWEEPS + 1):
                yhalo[stage, edge] = jnp.zeros((cx, nz), jnp.float32)

    half = nb // 2
    cuts = px_send.shape[0] // half
    place, side = b // 2, lax.rem(b, 2)
    other = 1 - side
    lanes = key_ref.shape[1]
    def pair_at(q):
        return lax.rem(place + q + 1, half) * 2


    def base_of(j):
        return (pair_at(j) + jnp.where(j < half, side, other)) * cr

    def spread_onehot(j):
        down = lax.broadcasted_iota(jnp.int32, (cr, lanes), 0) + base_of(j)
        for a in range(key_ref.shape[0]):
            hit = jnp.broadcast_to(key_ref[a : a + 1, :], (cr, lanes)) == down
            spread[j, :, a * lanes : (a + 1) * lanes] = jnp.where(hit, 1.0, 0.0).astype(jnp.bfloat16)

    def key_columns():
        for a in range(key_ref.shape[0]):
            wide = jnp.broadcast_to(key_ref[a : a + 1, :], (lanes, lanes)).astype(jnp.float32)
            keycol[a * lanes : (a + 1) * lanes, :] = wide.T.astype(jnp.int32)

    def gather_onehot(j):
        across = lax.broadcasted_iota(jnp.int32, (lanes, cr), 1) + base_of(j)
        for a in range(key_ref.shape[0]):
            hit = keycol[a * lanes : (a + 1) * lanes, :cr] == across
            gather[j, a * lanes : (a + 1) * lanes, :] = jnp.where(hit, 1.0, 0.0).astype(jnp.bfloat16)

    def x_copies(ref, sends, recvs, lead):
        def made(source, target, index, step):
            return pltpu.make_async_remote_copy(
                src_ref=ref.at[*lead, source, body_rows], dst_ref=ref.at[*lead, target, body_rows],
                send_sem=sends.at[*lead, index], recv_sem=recvs.at[*lead, index],
                device_id={"bulk": b + step}, device_id_type=pl.DeviceIdType.MESH,
            )
        return made(cx, 0, 0, 1), made(1, cx + 1, 1, -1)

    def y_copies(source, target, sends, recvs, lead):
        def made(side, index, step):
            return pltpu.make_async_remote_copy(
                src_ref=source.at[*lead, side], dst_ref=target.at[*lead, 1 - side],
                send_sem=sends.at[*lead, index], recv_sem=recvs.at[*lead, index],
                device_id={"slab": s + step}, device_id_type=pl.DeviceIdType.MESH,
            )
        return made(1, 2, 1), made(0, 3, -1)

    def copies_of(stage):
        lead = (stage,)
        return x_copies(v, send_sem, recv_sem, lead) + y_copies(ysend, yhalo, send_sem, recv_sem, lead)

    def k_copies():
        return x_copies(k, ksend_sem, krecv_sem, ()) + y_copies(kysend, kyhalo, ksend_sem, krecv_sem, ())

    to = (has[1], has[0], has[3], has[2])
    origin = (has[0], has[1], has[2], has[3])

    def start_all(copies):
        for there, copy in zip(to, copies):
            pl.when(there)(copy.start)

    def recv_all(copies):
        for there, copy in zip(origin, copies):
            pl.when(there)(copy.wait_recv)

    def send_all(copies):
        for there, copy in zip(to, copies):
            pl.when(there)(copy.wait_send)

    def stage_rows(ref, lead, target):
        for x in range(cx):
            target[*lead, 0, x : x + 1] = ref[*lead, x + 1, PAD : PAD + 1]
            target[*lead, 1, x : x + 1] = ref[*lead, x + 1, PAD + cy - 1 : PAD + cy]

    def place_rows(source, lead, ref):
        for x in range(cx):
            ref[*lead, x + 1, PAD - 1 : PAD] = source[*lead, 0, x : x + 1]
            ref[*lead, x + 1, PAD + cy : PAD + cy + 1] = source[*lead, 1, x : x + 1]

    def planes(body, unroll):
        def step(x, carry):
            body(x)
            return carry

        lax.fori_loop(1, cx - 1, step, 0, unroll=unroll)

    def x_edges(body):
        body(0, 0, cy)
        body(cx - 1, 0, cy)

    def y_edges(body, depth):
        def both(x):
            body(x, 0, depth)
            body(x, cy - depth, depth)

        planes(both, True)

    def interior(body, depth):
        planes(lambda x: body(x, depth, cy - 2 * depth), 7)

    loads[0].wait()
    stage_rows(v, (0,), ysend)
    loads[1].wait()
    stage_rows(k, (), kysend)

    pl.semaphore_wait(barrier, nb - 1 + has[2].astype(jnp.int32) + has[3].astype(jnp.int32))

    start_all(k_copies())
    start_all(copies_of(0))
    loads[4].wait()

    def coefficients(x, y, ny):
        own = slice(PAD + y, PAD + y + ny)
        at = slice(y, y + ny)
        here = k[x + 1, own]
        west = 0.5 * (here + k[x, own])
        east = 0.5 * (here + k[x + 2, own])
        south = 0.5 * (here + k[x + 1, PAD + y - 1 : PAD + y - 1 + ny])
        north = 0.5 * (here + k[x + 1, PAD + y + 1 : PAD + y + 1 + ny])
        lower = 0.5 * (here + jnp.where(first[:ny], 0.0, pltpu.roll(here, 1, 1)))
        upper = 0.5 * (here + jnp.where(last[:ny], 0.0, pltpu.roll(here, nz - 1, 1)))
        total = west + east + south + north + lower + upper
        fw[x, at] = west
        fw[x + 1, at] = east
        fs[x, at] = south
        fn[x, at] = north
        fl[x, at] = jnp.where(first[:ny], 0.0, lower)
        fu[x, at] = jnp.where(last[:ny], 0.0, upper)
        diag[x, at] = total
        dinv[x, at] = DAMPING / total

    def around(stage, x, y, ny):
        own = slice(PAD + y, PAD + y + ny)
        at = slice(y, y + ny)
        here = v[stage, x + 1, own]
        total = rhs[x, at] + fw[x, at] * v[stage, x, own] + fw[x + 1, at] * v[stage, x + 2, own]
        total = total + fs[x, at] * v[stage, x + 1, PAD + y - 1 : PAD + y - 1 + ny]
        total = total + fn[x, at] * v[stage, x + 1, PAD + y + 1 : PAD + y + 1 + ny]
        total = total + fl[x, at] * pltpu.roll(here, 1, 1) + fu[x, at] * pltpu.roll(here, nz - 1, 1)
        return total, here

    def smooth(stage):
        def body(x, y, ny):
            total, here = around(stage, x, y, ny)
            at = slice(y, y + ny)
            v[stage + 1, x + 1, PAD + y : PAD + y + ny] = (1 - DAMPING) * here + dinv[x, at] * total

        return body

    def residual(x, y, ny):
        total, here = around(SWEEPS, x, y, ny)
        start = x * cy + y
        if not isinstance(x, int):
            start = pl.multiple_of(start, 2 * PAD)
        rp[pl.ds(start, ny), :] = pieces_of(total - diag[x, y : y + ny] * here)

    def finish(x, y, ny):
        at = slice(y, y + ny)
        total, here = around(2 * SWEEPS, x, y, ny)
        out_ref[x, at] = (1 - DAMPING) * here + dinv[x, at] * total

    def halo_in(stage):
        recv_all(copies_of(stage))
        place_rows(yhalo, (stage,), v)

    def edges_out(body, stage):
        copies = copies_of(stage)
        x_edges(body)
        for there, copy in zip(to[:2], copies[:2]):
            pl.when(there)(copy.start)
        y_edges(body, PAD)
        stage_rows(v, (stage,), ysend)
        for there, copy in zip(to[2:], copies[2:]):
            pl.when(there)(copy.start)

    def sweep_on(stage):
        body = smooth(stage)
        interior(body, PAD)
        halo_in(stage)
        edges_out(body, stage + 1)

    interior(coefficients, PAD)
    interior(smooth(0), PAD)
    recv_all(k_copies())
    place_rows(kyhalo, (), k)
    x_edges(coefficients)
    y_edges(coefficients, PAD)
    halo_in(0)
    edges_out(smooth(0), 1)
    loads[2].wait()
    loads[3].wait()
    key_ref[...] = key_ref[...] * cr + row_key[...]
    each(nb, spread_onehot)
    for stage in range(1, SWEEPS):
        sweep_on(stage)

    interior(residual, 2 * PAD)
    key_columns()
    halo_in(SWEEPS)
    x_edges(residual)
    y_edges(residual, 2 * PAD)

    def piece(ref, first_slot, n):
        size = cr // cuts
        return ref.at[first_slot + n // cuts, pl.ds((n % cuts) * size, size)]

    def pair_copy(source, target, n, sends, recvs):
        return pltpu.make_async_remote_copy(
            src_ref=source, dst_ref=target, send_sem=sends.at[n], recv_sem=recvs.at[n],
            device_id={"bulk": 2 * place + other}, device_id_type=pl.DeviceIdType.MESH,
        )

    def far_copy(source, target, q, n, sends, recvs):
        return pltpu.make_async_remote_copy(
            src_ref=source, dst_ref=target, send_sem=sends.at[n], recv_sem=recvs.at[n],
            device_id={"bulk": pair_at(q) + side}, device_id_type=pl.DeviceIdType.MESH,
        )

    def px_copy(n):
        return pair_copy(piece(part, half, n), piece(crossed, 0, n), n, px_send, px_recv)

    def rs_copy(n):
        return far_copy(piece(part, 0, n), piece(arrived, 0, n), n // cuts, n, rs_send, rs_recv)

    group = 2 if half % 2 == 0 else 1

    def scatter(first_slot):
        hot = spread[pl.ds(first_slot, group)].reshape(group * cr, rows)
        product = jnp.dot(hot, rp[...], preferred_element_type=jnp.float32)
        part[pl.ds(first_slot, group)] = joined(product, nz).reshape(group, cr, nz)

    def scatter_across(g):
        scatter(half + g * group)
        each(group * cuts, lambda i: px_copy(g * group * cuts + i).start())

    each(half // group, scatter_across)
    each(half // group, lambda g: scatter(g * group))

    loads[5].wait()
    loads[6].wait()
    zc = lax.broadcasted_iota(jnp.int32, (cr, nz), 1)
    link = link_ref[...]
    below = jnp.where(zc == 0, 0.0, pltpu.roll(link, 1, 1))
    cinv = DAMPING / (leak_ref[...] + link + below)
    above = jnp.where(zc == nz - 1, 0.0, link)

    def pass_on(n):
        px_copy(n).wait_recv()
        rows_of = pl.ds((n % cuts) * (cr // cuts), cr // cuts)
        part[n // cuts, rows_of] = part[n // cuts, rows_of] + crossed[n // cuts, rows_of]
        rs_copy(n).start()

    own = (half - 1) * cuts
    each(own, pass_on)
    each(half, gather_onehot)
    each(cuts, lambda h: px_copy(own + h).wait_recv())
    coarse = part[half - 1] + crossed[half - 1]
    each(own, lambda n: rs_copy(n).wait_recv())
    if half <= 8:
        for q in range(half - 1):
            coarse = coarse + arrived[q]
    else:
        coarse = lax.fori_loop(0, half - 1, lambda q, total: total + arrived[q], coarse)

    u = cinv * coarse
    for sweep in range(COARSE_SWEEPS - 1):
        u = (1 - DAMPING) * u + cinv * (
            coarse + above * pltpu.roll(u, nz - 1, 1) + below * pltpu.roll(u, 1, 1)
        )
    corr[half - 1] = u

    def ag_copy(n):
        q, h = n // cuts, (n % cuts)
        slot = (half - 2 - q) * cuts + h
        return far_copy(piece(corr, 0, own + h), piece(corr, 0, slot), q, slot, ag_send, ag_recv)

    def cx_copy(n):
        return pair_copy(piece(corr, 0, n), piece(corr, half, n), n, cx_send, cx_recv)

    each(cuts, lambda h: cx_copy(own + h).start())
    each(own, lambda n: ag_copy(n).start())
    each(half, lambda q: gather_onehot(half + q))

    def hand_over(n):
        ag_copy(n).wait_recv()
        cx_copy((half - 2 - n // cuts) * cuts + (n % cuts)).start()

    each(own, hand_over)

    def collect(first_slot, fresh, spans=((0, rows),), between=()):
        values = pieces_of(corr[pl.ds(first_slot, group)].reshape(group * cr, nz))
        for index, (low, high) in enumerate(spans):
            hot = jnp.concatenate([gather[first_slot + i, low:high] for i in range(group)], axis=1)
            product = joined(jnp.dot(hot, values, preferred_element_type=jnp.float32), nz)
            acc[low:high] = product if fresh else acc[low:high] + product
            if index < len(between):
                between[index]()

    collect(half - group, True)
    each(half // group - 1, lambda g: collect(half - (g + 2) * group, False))

    def collect_crossed(g, *order):
        low = half - (g + 1) * group
        each(group * cuts, lambda i: cx_copy(low * cuts + i).wait_recv())
        collect(half + low, False, *order)

    each(half // group - 1, collect_crossed)

    def corrected(x, y, ny):
        start = x * cy + y
        if not isinstance(x, int):
            start = pl.multiple_of(start, PAD)
        own = slice(PAD + y, PAD + y + ny)
        v[SWEEPS + 1, x + 1, own] = v[SWEEPS, x + 1, own] + acc[pl.ds(start, ny), :]

    copies = copies_of(SWEEPS + 1)

    def send_x():
        x_edges(corrected)
        for there, copy in zip(to[:2], copies[:2]):
            pl.when(there)(copy.start)

    collect_crossed(
        half // group - 1, ((0, cy), (rows - cy, rows), (cy, rows - cy)), (lambda: None, send_x)
    )
    y_edges(corrected, PAD)
    stage_rows(v, (SWEEPS + 1,), ysend)
    for there, copy in zip(to[2:], copies[2:]):
        pl.when(there)(copy.start)
    interior(corrected, PAD)
    for stage in range(SWEEPS + 1, 2 * SWEEPS):
        sweep_on(stage)

    interior(finish, PAD)
    halo_in(2 * SWEEPS)
    x_edges(finish)
    y_edges(finish, PAD)

    send_all(k_copies())
    for stage in range(2 * SWEEPS + 1):
        send_all(copies_of(stage))
    each(half * cuts, lambda n: px_copy(n).wait_send())
    each(half * cuts, lambda n: cx_copy(n).wait_send())
    each(own, lambda n: rs_copy(n).wait_send())
    each(own, lambda n: ag_copy(n).wait_send())


def hand_back(parts, source, target, sems):
    size = source.shape[0] // parts
    copies = [
        pltpu.make_async_copy(
            source.at[pl.ds(i * size, size)], target.at[pl.ds(i * size, size)], sems.at[i]
        )
        for i in range(parts)
    ]
    for copy in copies:
        copy.start()
    for copy in copies:
        copy.wait()


def per_device(nb, ns, pressure, rhs, kappa, owner, coarse_row, coarse_leak, coarse_link):
    cx, cy, nz = pressure.shape
    cr = coarse_leak.shape[1]
    rows = cx * cy
    lanes = 128
    cuts = 2 if cr % 16 == 0 else 1
    keys = (rows // lanes, lanes)
    parts = 4 if cx % 4 == 0 else 1
    stages = 2 * SWEEPS + 1
    f32, bf16 = jnp.float32, jnp.bfloat16
    block = (cx, cy, nz)
    padded = (cx + 2, cy + 2 * PAD, nz)
    vmem = pl.BlockSpec(memory_space=pltpu.VMEM)
    hbm = pl.BlockSpec(memory_space=pltpu.HBM)
    dma = pltpu.SemaphoreType.DMA
    result = pl.pallas_call(
        functools.partial(kernel, nb, ns),
        out_shape=pltpu.VMEM(block, f32),
        in_specs=[hbm] * 7,
        out_specs=vmem,
        scratch_shapes=[
            pltpu.VMEM(keys, jnp.int32),
            pltpu.VMEM(keys, jnp.int32),
            pltpu.VMEM((cr, nz), f32),
            pltpu.VMEM((cr, nz), f32),
            pltpu.VMEM((stages,) + padded, f32),
            pltpu.VMEM(padded, f32),
            pltpu.VMEM(block, f32),
            pltpu.VMEM((cx + 1, cy, nz), f32),
            pltpu.VMEM(block, f32),
            pltpu.VMEM(block, f32),
            pltpu.VMEM(block, f32),
            pltpu.VMEM(block, f32),
            pltpu.VMEM(block, f32),
            pltpu.VMEM(block, f32),
            pltpu.VMEM((stages, 2, cx, nz), f32),
            pltpu.VMEM((stages, 2, cx, nz), f32),
            pltpu.VMEM((2, cx, nz), f32),
            pltpu.VMEM((2, cx, nz), f32),
            pltpu.VMEM((nb, cr, rows), bf16),
            pltpu.VMEM((nb, rows, cr), bf16),
            pltpu.VMEM((rows, lanes), jnp.int32),
            pltpu.VMEM((rows, PIECES * nz), bf16),
            pltpu.VMEM((nb, cr, nz), f32),
            pltpu.VMEM((nb // 2, cr, nz), f32),
            pltpu.VMEM((nb // 2, cr, nz), f32),
            pltpu.VMEM((nb, cr, nz), f32),
            pltpu.VMEM((rows, nz), f32),
            dma((7,)),
            dma((stages, 4)),
            dma((stages, 4)),
            dma((4,)),
            dma((4,)),
            dma((nb // 2 * cuts,)),
            dma((nb // 2 * cuts,)),
            dma((nb // 2 * cuts,)),
            dma((nb // 2 * cuts,)),
            dma((nb // 2 * cuts,)),
            dma((nb // 2 * cuts,)),
            dma((nb // 2 * cuts,)),
            dma((nb // 2 * cuts,)),
        ],
        compiler_params=pltpu.CompilerParams(
            collective_id=0, has_side_effects=True, vmem_limit_bytes=58 * 2**20
        ),
    )(
        owner.reshape(keys), coarse_row.reshape(keys), pressure, rhs, kappa,
        coarse_leak[0], coarse_link[0],
    )
    return pl.pallas_call(
        functools.partial(hand_back, parts),
        out_shape=jax.ShapeDtypeStruct(block, f32),
        in_specs=[vmem],
        out_specs=hbm,
        scratch_shapes=[dma((parts,))],
        compiler_params=pltpu.CompilerParams(vmem_limit_bytes=16 * 2**20),
    )(result)


def solution(mesh):
    return jax.shard_map(
        functools.partial(per_device, mesh.shape["bulk"], mesh.shape["slab"]),
        mesh=mesh,
        in_specs=(
            P("bulk", "slab", None),
            P("bulk", "slab", None),
            P("bulk", "slab", None),
            P("slab", "bulk", None, None),
            P("slab", "bulk", None),
            P("slab", "bulk", None),
            P("slab", "bulk", None),
        ),
        out_specs=P("bulk", "slab", None),
        check_vma=False,
    )
```
